512 devices in a mesh: hst: 64 (over z, y), local: 8 (over x, core).
Axes of the slice: x: 4, y: 8, z: 8, core: 2. Of those that a mesh axis runs over, the one named last changes fastest.
Arguments:
- checkpoint: bfloat16 [64, 8, 64, 256], P(None, 'local', 'hst'), may hold values from -0.1875 to 0.1875
- counts: int32 [64, 4096, 512], P('hst', None, 'local'), may hold values from 0 to 2
- table_host: int32 [64], replicated, may hold values from 0 to 63, each once
- stored_slot: int32 [64], replicated, may hold values from 0 to 63, each once
- owner_order: int32 [4096], replicated, may hold values from 0 to 4095, each once
- fm_proj: bfloat16 [2, 64, 12], replicated, may hold values from -0.75 to 0.75
- fm_weight: bfloat16 [2, 768, 8192], P(None, None, 'local'), may hold values from -0.21875 to 0.21875
- fm_gain: float32 [2, 768], replicated, may hold values from 0.5 to 1.5
- lin_weight: bfloat16 [2, 32, 64], replicated, may hold values from -0.75 to 0.75
- out_gain: float32 [2, 256], replicated, may hold values from 0.5 to 1.5
Outputs:
- features: bfloat16 [4096, 64, 256], P(('hst', 'local'))
The draws below stay inside these ranges and needn't reach their ends.
All inputs are finite; a program needn't handle non-finite values.
Results may differ from the reference program's by a relative error of at most 0.023.
Values may be sent and summed in bfloat16 or wider, within the bound.
No kernel may reach another device: no remote copies, remote signals or barrier semaphores. Data moves between devices by JAX's collectives and lax.ppermute only.
A program may use at most 64 MiB of HBM per device.

```python
import jax
import jax.numpy as jnp
from jax import lax

EMBED = 256
RANK = 12
ROWS_DEV = 64
LAYERS = 2
TABLES = 64
FM_OUT = 32
LIN_OUT = 32
BLOCKS = 8
ROWS = 512
BATCH = 4096


def plant(values, own_key, least, top_value):
    place = [jax.random.randint(jax.random.fold_in(own_key, axis), (), 0, length) for axis, length in enumerate(values.shape)]
    main_axis = values.shape.index(max(values.shape))
    neighbour = place[:main_axis] + [(place[main_axis] + 1) % values.shape[main_axis]] + place[main_axis + 1:]
    return values.at[tuple(place)].set(least).at[tuple(neighbour)].set(top_value)


def levels(key, dims, pieces, smallest, largest):
    level, own = 1.0, jax.random.fold_in(key, 6)
    for axis_at, blocks in pieces:
        heights = jnp.exp(jax.random.uniform(jax.random.fold_in(own, axis_at), (blocks,), jnp.float32, smallest / len(pieces), largest / len(pieces)))
        level = level * jnp.repeat(heights, dims[axis_at] // blocks).reshape([-1 if axis == axis_at else 1 for axis in range(len(dims))])
    return level


def bell_draw(key, shape, scale, most, cuts=(), kind=jnp.bfloat16):
    drawn = scale * jax.random.normal(key, shape, jnp.float32)
    if cuts:
        drawn = drawn * levels(key, shape, cuts, -0.22, 0.18)
    return jnp.clip(drawn, -most, most).astype(kind)


def setup_inputs(seed: int = 0) -> dict:
    streams_of = jax.random.split(jax.random.key(seed), 11)
    checkpoint = bell_draw(streams_of[0], (TABLES, BLOCKS, ROWS_DEV, EMBED), (2 * ROWS) ** -0.5, 0.1875, ((1, 8), (2, 64)))
    counts = plant(jax.random.randint(streams_of[1], (TABLES, BATCH, ROWS), 0, 3), jax.random.fold_in(streams_of[1], 1), 0, 2).astype(jnp.int32)
    table_host = jax.random.permutation(streams_of[2], TABLES).astype(jnp.int32)
    stored_slot = jax.random.permutation(streams_of[3], TABLES).astype(jnp.int32)
    owner_order = jax.random.permutation(streams_of[4], BATCH).astype(jnp.int32)
    fm_proj = bell_draw(streams_of[5], (LAYERS, TABLES, RANK), TABLES ** -0.5, 0.75)
    fm_weight = bell_draw(streams_of[6], (LAYERS, TABLES * RANK, FM_OUT * EMBED), (TABLES * RANK) ** -0.5, 0.21875, ((2, 8),))
    fm_gain = jnp.clip(1.0 + 0.1 * jax.random.normal(streams_of[7], (LAYERS, TABLES * RANK), jnp.float32), 0.5, 1.5)
    lin_weight = bell_draw(streams_of[8], (LAYERS, LIN_OUT, TABLES), TABLES ** -0.5, 0.75)
    out_gain = jnp.clip(1.0 + 0.1 * jax.random.normal(streams_of[9], (LAYERS, EMBED), jnp.float32), 0.5, 1.5)
    return {"checkpoint": checkpoint, "counts": counts, "table_host": table_host, "stored_slot": stored_slot, "owner_order": owner_order, "fm_proj": fm_proj, "fm_weight": fm_weight, "fm_gain": fm_gain, "lin_weight": lin_weight, "out_gain": out_gain}


def norm_rows(values, gain):
    mean = lax.optimization_barrier(jnp.mean(values, axis=-1, keepdims=True))
    centered = values - mean
    spread = lax.optimization_barrier(jnp.mean(centered * centered, axis=-1, keepdims=True))
    return centered * lax.rsqrt(spread + 1e-05) * gain

def wukong_layer(layer_state, projected_state, weight, gain, linear_output, out_scale):
    state_float = layer_state.astype(jnp.float32)
    inner_products = jnp.einsum('pud,uj->pdj', state_float, projected_state.astype(jnp.float32)).astype(jnp.bfloat16)
    interaction_matrix = jnp.einsum('ogx,oxl->ogl', state_float, inner_products.astype(jnp.float32))
    interaction_matrix = interaction_matrix.reshape(layer_state.shape[0], -1)
    flat = norm_rows(interaction_matrix, gain).astype(jnp.bfloat16)
    mixed = jnp.dot(flat, weight, preferred_element_type=jnp.float32).astype(jnp.bfloat16)
    mixed = mixed.reshape(layer_state.shape[0], -1, layer_state.shape[2])
    compressed_state = jnp.einsum('wp,jpo->jwo', linear_output.astype(jnp.float32), state_float)
    joined = jnp.concatenate([mixed.astype(jnp.float32), compressed_state], axis=1) + state_float
    return norm_rows(joined, out_scale).astype(jnp.bfloat16)

def reference(checkpoint, counts, table_host, stored_slot, owner_order, fm_proj, fm_weight, fm_gain, lin_weight, out_gain):

    def pool(table_id):
        table = checkpoint[stored_slot[table_id]].reshape(-1, checkpoint.shape[-1])
        bags = jnp.take(counts[table_host[table_id]], owner_order, axis=0).astype(jnp.bfloat16)
        return jnp.dot(bags, table, preferred_element_type=jnp.float32).astype(jnp.bfloat16)
    pooled = lax.map(pool, jnp.arange(TABLES, dtype=jnp.int32))
    layer_state = jnp.transpose(pooled, (1, 0, 2))
    for layer in range(LAYERS):
        layer_state = wukong_layer(layer_state, fm_proj[layer], fm_weight[layer], fm_gain[layer], lin_weight[layer], out_gain[layer])
    return layer_state
```

```python
import jax
import jax.numpy as jnp
from jax import lax
from jax.experimental import pallas as pl
from jax.experimental.pallas import tpu as pltpu
from jax.sharding import PartitionSpec as P

LAYERS = 2
PACK = 4
VMEM_LIMIT = 32 * 1024 * 1024


def one_hot_rows(rows, positions):
    number = lax.broadcasted_iota(jnp.int32, (rows, positions.shape[1]), 0)
    return jnp.where(number == positions, 1.0, 0.0).astype(jnp.bfloat16)


def pick_rows(host_ref, slot_ref, stored_ref, out_ref):
    tables = stored_ref.shape[0]
    holder = one_hot_rows(tables, host_ref[...])
    slot = one_hot_rows(tables, slot_ref[...])
    chosen = lax.dot_general(
        holder, slot, (((1,), (1,)), ((), ())), preferred_element_type=jnp.float32
    ).astype(jnp.bfloat16)
    out_ref[:, 0, :] = jnp.dot(chosen, stored_ref[...], preferred_element_type=jnp.float32)


def order_counts(counts_ref, order_ref, out_ref, packed_ref):
    rows, samples = counts_ref.shape
    words = rows // PACK
    low_count = 256
    high_count = samples // low_count
    word = counts_ref[0:words, :]
    for k in range(1, PACK):
        word = word + (counts_ref[k * words : (k + 1) * words, :] << (2 * k))
    word = word.astype(jnp.float32).astype(jnp.bfloat16)
    for high in range(high_count):
        packed_ref[high * words : (high + 1) * words, :] = word[
            :, high * low_count : (high + 1) * low_count
        ]
    for target in range(order_ref.shape[0]):
        number = order_ref[target : target + 1, :]
        high_part = number >> 8
        picked = jnp.dot(
            packed_ref[...],
            one_hot_rows(low_count, number & (low_count - 1)),
            preferred_element_type=jnp.float32,
        )
        value = jnp.zeros((words, number.shape[1]), jnp.float32)
        for high in range(high_count):
            value = value + jnp.where(
                high_part == high, picked[high * words : (high + 1) * words, :], 0.0
            )
        value = value.astype(jnp.int32)
        for k in range(PACK):
            out_ref[target, k * words : (k + 1) * words, :] = (
                ((value >> (2 * k)) & 3).astype(jnp.float32).astype(jnp.bfloat16)
            )


def call(kernel, out_shape, *args, scratch=()):
    return pl.pallas_call(
        kernel,
        out_shape=out_shape,
        in_specs=[pl.BlockSpec(memory_space=pltpu.VMEM)] * len(args),
        out_specs=pl.BlockSpec(memory_space=pltpu.VMEM),
        scratch_shapes=list(scratch),
        compiler_params=pltpu.CompilerParams(vmem_limit_bytes=VMEM_LIMIT),
    )(*args)


def gather_local(value):
    count = lax.axis_size("local")
    return lax.all_to_all(
        jnp.broadcast_to(value[None], (count, *value.shape)), "local", 0, 0, tiled=False
    )


def norm_rows(values, gain):
    mean = jnp.mean(values, axis=-1, keepdims=True)
    centered = values - mean
    spread = jnp.mean(centered * centered, axis=-1, keepdims=True)
    return centered * lax.rsqrt(spread + 1e-05) * gain


def wukong_layer(layer_state, projected_state, weight, gain, linear_output, out_scale):
    samples = layer_state.shape[0]
    inner_products = jnp.einsum(
        "pud,uj->pdj", layer_state, projected_state, preferred_element_type=jnp.float32
    ).astype(jnp.bfloat16)
    interaction_matrix = jnp.einsum(
        "ogx,oxl->ogl", layer_state, inner_products, preferred_element_type=jnp.float32
    )
    interaction_matrix = interaction_matrix.reshape(samples, -1)
    flat = norm_rows(interaction_matrix, gain).astype(jnp.bfloat16)
    gathered = gather_local(flat).reshape(-1, flat.shape[1])
    column_part = jnp.dot(gathered, weight, preferred_element_type=jnp.float32).astype(jnp.bfloat16)
    mixed = lax.all_to_all(column_part, "local", split_axis=0, concat_axis=1, tiled=True)
    mixed = mixed.reshape(samples, -1, layer_state.shape[2])
    compressed_state = jnp.einsum(
        "wp,jpo->jwo", linear_output, layer_state, preferred_element_type=jnp.float32
    )
    joined = jnp.concatenate(
        [mixed.astype(jnp.float32), compressed_state], axis=1
    ) + layer_state.astype(jnp.float32)
    return norm_rows(joined, out_scale).astype(jnp.bfloat16)


def shards(
    checkpoint,
    counts,
    table_host,
    stored_slot,
    owner_order,
    fm_proj,
    fm_weight,
    fm_gain,
    lin_weight,
    out_gain,
):
    hosts = lax.axis_size("hst")
    locals_ = lax.axis_size("local")
    width = checkpoint.shape[-1]
    tables = table_host.shape[0]
    batch = owner_order.shape[0]
    samples = batch // (hosts * locals_)
    rows = counts.shape[2]

    order = jnp.transpose(owner_order.reshape(hosts, locals_, samples), (1, 0, 2))
    ordered = call(
        order_counts,
        jax.ShapeDtypeStruct((locals_, rows, hosts * samples), jnp.bfloat16),
        jnp.transpose(counts[0]),
        order.reshape(locals_, hosts * samples),
        scratch=[pltpu.VMEM((batch // 256 * (rows // PACK), 256), jnp.bfloat16)],
    )
    bags = lax.all_to_all(ordered, "local", 0, 0, tiled=False)

    outgoing = call(
        pick_rows,
        jax.ShapeDtypeStruct((tables, 1, width), jnp.float32),
        table_host.reshape(1, tables),
        stored_slot.reshape(1, tables),
        checkpoint.reshape(tables, width),
    )
    arrived = lax.all_to_all(outgoing, "hst", 0, 0, tiled=False)
    table = gather_local(arrived.reshape(tables, width).astype(jnp.bfloat16))

    pooled = lax.dot_general(
        bags.reshape(-1, hosts * samples),
        table.reshape(-1, width),
        (((0,), (0,)), ((), ())),
        preferred_element_type=jnp.float32,
    ).astype(jnp.bfloat16)
    moved = lax.all_to_all(pooled.reshape(hosts, samples, width), "hst", 0, 0, tiled=False)
    layer_state = jnp.transpose(jnp.take(moved, table_host, axis=0), (1, 0, 2))
    for layer in range(LAYERS):
        layer_state = wukong_layer(
            layer_state,
            fm_proj[layer],
            fm_weight[layer],
            fm_gain[layer],
            lin_weight[layer],
            out_gain[layer],
        )
    return layer_state


def solution(mesh):
    placed = (
        P(None, "local", "hst", None),
        P("hst", None, "local"),
        P(),
        P(),
        P(),
        P(),
        P(None, None, "local"),
        P(),
        P(),
        P(),
    )
    return jax.shard_map(
        shards,
        mesh=mesh,
        in_specs=placed,
        out_specs=P(("hst", "local"), None, None),
        check_vma=False,
    )
```

```python
import jax
import jax.numpy as jnp
from jax import lax
from jax.experimental import pallas as pl
from jax.experimental.pallas import tpu as pltpu
from jax.sharding import PartitionSpec as P

LAYERS = 2
PACK = 4
LOW = 256
LANES = 128
VMEM_LIMIT = 40 * 1024 * 1024
F32 = jnp.float32
BF16 = jnp.bfloat16


def number(shape, axis):
    return lax.broadcasted_iota(jnp.int32, shape, axis)


def ones_where(condition):
    return jnp.where(condition, 1.0, 0.0).astype(BF16)


def matmul(a, b):
    return jnp.dot(a, b, preferred_element_type=F32)


def matmul_nt(a, b):
    return lax.dot_general(a, b, (((1,), (1,)), ((), ())), preferred_element_type=F32)


def matmul_tn(a, b):
    return lax.dot_general(a, b, (((0,), (0,)), ((), ())), preferred_element_type=F32)


def pick_rows(host_ref, slot_ref, stored_ref, out_ref):
    tables = stored_ref.shape[0]
    holder = ones_where(number((tables, tables), 0) == host_ref[...])
    slot = ones_where(number((tables, tables), 0) == slot_ref[...])
    chosen = matmul_nt(holder, slot).astype(BF16)
    out_ref[:, 0, :] = matmul(chosen, stored_ref[...])


def order_counts(after_ref, counts_ref, order_ref, out_ref, packed_ref):
    rows, batch = counts_ref.shape
    targets, _, length = out_ref.shape
    words = rows // PACK
    high_count = batch // LOW
    order_rows = order_ref.shape[0]
    samples = 8
    word = counts_ref[0:words, :]
    for k in range(1, PACK):
        word = word + (counts_ref[k * words : (k + 1) * words, :] << (2 * k))
    word = word.astype(F32).astype(BF16)
    for high in range(high_count):
        packed_ref[high * words : (high + 1) * words, :] = word[:, high * LOW : (high + 1) * LOW]
    order = order_ref[...]
    parts = jnp.concatenate([order >> 8, order & (LOW - 1)], axis=0).astype(F32).astype(BF16)
    for target in range(targets):
        m = number((LANES, length), 1)
        row = (m // samples) * (targets * samples) + target * samples + m % samples
        found = matmul(parts, ones_where(number((LANES, length), 0) == row % LANES))
        m = number((2 * order_rows, length), 1)
        row = (m // samples) * (targets * samples) + target * samples + m % samples
        found = jnp.where(
            number((2 * order_rows, length), 0) % order_rows == row // LANES, found, 0.0
        )
        high_part = jnp.sum(found[:order_rows], axis=0, keepdims=True).astype(jnp.int32)
        low_part = jnp.sum(found[order_rows:], axis=0, keepdims=True).astype(jnp.int32)
        picked = matmul(packed_ref[...], ones_where(number((LOW, length), 0) == low_part))
        value = jnp.zeros((words, length), F32)
        for high in range(high_count):
            value = value + jnp.where(
                high_part == high, picked[high * words : (high + 1) * words, :], 0.0
            )
        value = value.astype(jnp.int32)
        for k in range(PACK):
            out_ref[target, k * words : (k + 1) * words, :] = (
                ((value >> (2 * k)) & 3).astype(F32).astype(BF16)
            )


def join_table(arrived_ref, ordered_ref, out_ref):
    length = ordered_ref.shape[2]
    table = arrived_ref[:, 0, :].astype(BF16)
    for target in range(out_ref.shape[0]):
        out_ref[target, :, :length] = ordered_ref[target]
        out_ref[target, :, length:] = table


def pool(both_ref, out_ref):
    length = out_ref.shape[0]
    out_ref[...] = matmul_tn(both_ref[:, :length], both_ref[:, length:]).astype(BF16)


def spread(rows, columns, samples, of_rows):
    if of_rows:
        return ones_where(number((rows, columns), 0) // samples == number((rows, columns), 1))
    return ones_where(number((rows, columns), 1) // samples == number((rows, columns), 0))


def same_sample(rows, columns, samples):
    return number((rows, columns), 0) % samples == number((rows, columns), 1) % samples


def prepare(
    after_ref, host_ref, proj_ref, lin_ref, weight_ref, gain_ref,
    place_ref, proj_out_ref, lin_out_ref, weight_out_ref, gain_out_ref,
):
    layers, rank, tables = proj_ref.shape
    state = place_ref.shape[0]
    samples = state // tables
    flat = gain_ref.shape[1]
    ranks = flat // tables
    wide = spread(tables, state, samples, False)
    holder = ones_where(number((tables, tables), 0) == host_ref[...])
    chosen = matmul_nt(spread(state, tables, samples, True), holder).astype(BF16)
    place = matmul(chosen, wide)
    place_ref[...] = jnp.where(same_sample(state, state, samples), place, 0.0).astype(BF16)
    row = number((flat, flat), 0)
    turn = ones_where((row % tables) * ranks + row // tables == number((flat, flat), 1))
    column = number((flat, flat), 1)
    turn_back = ones_where((column % tables) * ranks + column // tables == number((flat, flat), 0))
    gain = gain_ref[...]
    total = jnp.zeros(gain.shape, F32)
    for _ in range(3):
        part = gain.astype(BF16)
        total = total + matmul(part, turn_back)
        gain = gain - part.astype(F32)
    gain_out_ref[...] = total
    for layer in range(layers):
        tall = spread(proj_out_ref.shape[1], rank, samples, True)
        values = matmul(matmul(tall, proj_ref[layer]).astype(BF16), wide)
        keep = same_sample(proj_out_ref.shape[1], state, samples)
        proj_out_ref[layer] = jnp.where(keep, values, 0.0).astype(BF16)
        tall = spread(lin_out_ref.shape[1], lin_ref.shape[1], samples, True)
        values = matmul(matmul(tall, lin_ref[layer]).astype(BF16), wide)
        keep = same_sample(lin_out_ref.shape[1], state, samples)
        lin_out_ref[layer] = jnp.where(keep, values, 0.0).astype(BF16)
        for start in range(0, weight_ref.shape[2], 256):
            weight_out_ref[layer, :, start : start + 256] = matmul(
                turn, weight_ref[layer, :, start : start + 256]
            ).astype(BF16)


def norm_rows(values, gain):
    mean = jnp.mean(values, axis=-1, keepdims=True)
    centered = values - mean
    spread_ = jnp.mean(centered * centered, axis=-1, keepdims=True)
    return centered * lax.rsqrt(spread_ + 1e-05) * gain


def by_sample(state):
    rows = state.shape[0]
    samples = 8
    row = number((rows, rows), 0)
    tables = rows // samples
    turn = ones_where((row % tables) * samples + row // tables == number((rows, rows), 1))
    return matmul(turn, state).astype(BF16)


def interactions(state, turned, proj, gain, flat_ref):
    rows = state.shape[0]
    samples = flat_ref.shape[1]
    tables = rows // samples
    inner = matmul(proj, state).astype(BF16)
    inter = matmul_nt(inner, turned)
    own = number(inter.shape, 0) % samples == number(inter.shape, 1) // tables
    inter = jnp.where(own, inter, 0.0)
    while inter.shape[1] > LANES:
        half = inter.shape[1] // 2
        inter = inter[:, :half] + inter[:, half:]
    inter = inter + pltpu.roll(inter, tables, 1)
    first = number((samples, LANES), 1) < tables
    flat = jnp.concatenate(
        [
            jnp.where(first, inter[at : at + samples], inter[at + samples : at + 2 * samples])
            for at in range(0, inter.shape[0], 2 * samples)
        ],
        axis=1,
    )
    flat = norm_rows(flat, gain).astype(BF16)
    for target in range(flat_ref.shape[0]):
        flat_ref[target] = flat


def first_layer(moved_ref, place_ref, proj_ref, gain_ref, state_ref, flat_ref):
    state = matmul(place_ref[...], moved_ref[...]).astype(BF16)
    state_ref[...] = state
    interactions(state, by_sample(state), proj_ref[0], gain_ref[0:1, :], flat_ref)


def map_columns(layer, flat_ref, weight_ref, out_ref):
    out_ref[...] = matmul(flat_ref[...], weight_ref[layer]).astype(BF16)


def next_state(mixed_ref, state, lin, scale):
    width = state.shape[1]
    compressed = matmul(lin, state)
    mixed = [
        mixed_ref[source, :, start : start + width].astype(F32)
        for source in range(mixed_ref.shape[0])
        for start in range(0, mixed_ref.shape[2], width)
    ]
    joined = jnp.concatenate([*mixed, compressed], axis=0) + state.astype(F32)
    return norm_rows(joined, scale).astype(BF16)


def next_layer(layer, mixed_ref, old_ref, lin_ref, scale_ref, proj_ref, gain_ref, state_ref, flat_ref):
    state = next_state(mixed_ref, old_ref[...], lin_ref[layer], scale_ref[layer : layer + 1, :])
    state_ref[...] = state
    interactions(
        state, by_sample(state), proj_ref[layer + 1], gain_ref[layer + 1 : layer + 2, :], flat_ref
    )


def last_state(layer, mixed_ref, old_ref, lin_ref, scale_ref, out_ref):
    out_ref[...] = by_sample(
        next_state(mixed_ref, old_ref[...], lin_ref[layer], scale_ref[layer : layer + 1, :])
    )


def call(kernel, out_shape, *args, after=(), scratch=(), flops=0):
    moved = sum(a.size * a.dtype.itemsize for a in args)
    return pl.pallas_call(
        kernel,
        out_shape=out_shape,
        in_specs=[pl.BlockSpec(memory_space=pl.ANY)] * len(after)
        + [pl.BlockSpec(memory_space=pltpu.VMEM)] * len(args),
        out_specs=jax.tree.map(lambda _: pl.BlockSpec(memory_space=pltpu.VMEM), out_shape),
        scratch_shapes=list(scratch),
        compiler_params=pltpu.CompilerParams(vmem_limit_bytes=VMEM_LIMIT),
        cost_estimate=pl.CostEstimate(flops=flops, bytes_accessed=moved, transcendentals=0),
    )(*after, *args)


def exchange(value, axis):
    return lax.all_to_all(value, axis, 0, 0, tiled=False)


def shards(
    checkpoint,
    counts,
    table_host,
    stored_slot,
    owner_order,
    fm_proj,
    fm_weight,
    fm_gain,
    lin_weight,
    out_gain,
):
    hosts = lax.axis_size("hst")
    locals_ = lax.axis_size("local")
    width = checkpoint.shape[-1]
    tables = table_host.shape[0]
    batch = owner_order.shape[0]
    samples = batch // (hosts * locals_)
    rows = counts.shape[2]
    length = hosts * samples
    state_rows = tables * samples
    rank = fm_proj.shape[2]
    flat_size = tables * rank
    lin_rows = lin_weight.shape[1] * samples

    def shape(dims, dtype=BF16):
        return jax.ShapeDtypeStruct(dims, dtype)

    outgoing = call(
        pick_rows,
        shape((tables, 1, width), F32),
        table_host.reshape(1, tables),
        stored_slot.reshape(1, tables),
        checkpoint.reshape(tables, width),
    )
    arrived = exchange(outgoing, "hst")
    ordered = call(
        order_counts,
        shape((locals_, rows, length)),
        jnp.transpose(counts[0]),
        owner_order.reshape(batch // LANES, LANES),
        after=(outgoing,),
        scratch=[pltpu.VMEM((batch // LOW * (rows // PACK), LOW), BF16)],
        flops=2 * batch * (LOW * LOW + 64 * LANES),
    )
    both = exchange(
        call(join_table, shape((locals_, rows, length + width)), arrived, ordered), "local"
    )
    pooled = call(pool, shape((length, width)), both.reshape(locals_ * rows, length + width))
    moved = exchange(pooled.reshape(hosts, samples, width), "hst")

    proj_rows = -(-rank // 16) * 16
    place, proj, lin, weight, gain = call(
        prepare,
        (
            shape((state_rows, state_rows)),
            shape((LAYERS, rank * samples, state_rows)),
            shape((LAYERS, lin_rows, state_rows)),
            shape(fm_weight.shape),
            shape(fm_gain.shape, F32),
        ),
        table_host.reshape(1, tables),
        jnp.pad(jnp.transpose(fm_proj, (0, 2, 1)), ((0, 0), (0, proj_rows - rank), (0, 0))),
        lin_weight,
        fm_weight,
        fm_gain,
        after=(pooled,),
        flops=2 * 2 * flat_size * flat_size * fm_weight.shape[2],
    )
    flat_shape = shape((locals_, samples, flat_size))
    state, flat = call(
        first_layer,
        (shape((state_rows, width)), flat_shape),
        moved.reshape(state_rows, width),
        place,
        proj,
        gain,
    )
    for layer in range(LAYERS):
        gathered = exchange(flat, "local").reshape(locals_ * samples, flat_size)
        columns = call(
            lambda *refs, layer=layer: map_columns(layer, *refs),
            shape((locals_ * samples, fm_weight.shape[2])),
            gathered,
            weight,
        )
        mixed = exchange(columns.reshape(locals_, samples, -1), "local")
        if layer + 1 < LAYERS:
            state, flat = call(
                lambda *refs, layer=layer: next_layer(layer, *refs),
                (shape((state_rows, width)), flat_shape),
                mixed,
                state,
                lin,
                out_gain,
                proj,
                gain,
            )
        else:
            state = call(
                lambda *refs, layer=layer: last_state(layer, *refs),
                shape((state_rows, width)),
                mixed,
                state,
                lin,
                out_gain,
            )
    return state.reshape(samples, tables, width)


def solution(mesh):
    placed = (
        P(None, "local", "hst", None),
        P("hst", None, "local"),
        P(),
        P(),
        P(),
        P(),
        P(None, None, "local"),
        P(),
        P(),
        P(),
    )
    return jax.shard_map(
        shards,
        mesh=mesh,
        in_specs=placed,
        out_specs=P(("hst", "local"), None, None),
        check_vma=False,
    )
```

```python
import jax
import jax.numpy as jnp
from jax import lax
from jax.experimental import pallas as pl
from jax.experimental.pallas import tpu as pltpu
from jax.sharding import PartitionSpec as P

LAYERS = 2
PACK = 4
LOW = 256
LANES = 128
SMALL, MIDDLE, LARGE = 40 << 20, 49 << 20, 60 << 20
F32 = jnp.float32
BF16 = jnp.bfloat16


def number(shape, axis):
    return lax.broadcasted_iota(jnp.int32, shape, axis)


def ones_where(condition):
    return jnp.where(condition, 1.0, 0.0).astype(BF16)


def matmul(a, b):
    return jnp.dot(a, b, preferred_element_type=F32)


def matmul_nt(a, b):
    return lax.dot_general(a, b, (((1,), (1,)), ((), ())), preferred_element_type=F32)


def matmul_tn(a, b):
    return lax.dot_general(a, b, (((0,), (0,)), ((), ())), preferred_element_type=F32)


def fetch(pairs, sems):
    copies = [pltpu.make_async_copy(source, target, sems.at[at]) for at, (source, target) in enumerate(pairs)]
    for copy in copies:
        copy.start()
    return copies


def pick_rows(host_hbm, slot_hbm, stored_hbm, out_ref, host_ref, slot_ref, stored_ref, sems):
    for copy in fetch([(host_hbm, host_ref), (slot_hbm, slot_ref), (stored_hbm, stored_ref)], sems):
        copy.wait()
    tables = stored_ref.shape[0]
    holder = ones_where(number((tables, tables), 0) == host_ref[...])
    slot = ones_where(number((tables, tables), 0) == slot_ref[...])
    chosen = matmul_nt(holder, slot).astype(BF16)
    out_ref[:, 0, :] = matmul(chosen, stored_ref[...])


def order_counts(counts_ref, order_ref, out_ref, packed_ref):
    rows, batch = counts_ref.shape
    targets, _, length = out_ref.shape
    words = rows // PACK
    high_count = batch // LOW
    order_rows = order_ref.shape[0]
    samples = 8
    word = counts_ref[0:words, :]
    for k in range(1, PACK):
        word = word + (counts_ref[k * words : (k + 1) * words, :] << (2 * k))
    word = word.astype(F32).astype(BF16)
    for high in range(high_count):
        packed_ref[high * words : (high + 1) * words, :] = word[:, high * LOW : (high + 1) * LOW]
    order = order_ref[...]
    parts = jnp.concatenate([order >> 8, order & (LOW - 1)], axis=0).astype(F32).astype(BF16)
    for target in range(targets):
        m = number((LANES, length), 1)
        row = (m // samples) * (targets * samples) + target * samples + m % samples
        found = matmul(parts, ones_where(number((LANES, length), 0) == row % LANES))
        m = number((2 * order_rows, length), 1)
        row = (m // samples) * (targets * samples) + target * samples + m % samples
        found = jnp.where(
            number((2 * order_rows, length), 0) % order_rows == row // LANES, found, 0.0
        )
        high_part = jnp.sum(found[:order_rows], axis=0, keepdims=True).astype(jnp.int32)
        low_part = jnp.sum(found[order_rows:], axis=0, keepdims=True).astype(jnp.int32)
        picked = matmul(packed_ref[...], ones_where(number((LOW, length), 0) == low_part))
        value = jnp.zeros((words, length), F32)
        for high in range(high_count):
            value = value + jnp.where(
                high_part == high, picked[high * words : (high + 1) * words, :], 0.0
            )
        value = value.astype(jnp.int32)
        for k in range(PACK):
            out_ref[target, k * words : (k + 1) * words, :] = (
                ((value >> (2 * k)) & 3).astype(F32).astype(BF16)
            )


def join_table(arrived_ref, ordered_ref, out_ref):
    length = ordered_ref.shape[2]
    table = arrived_ref[:, 0, :].astype(BF16)
    for target in range(out_ref.shape[0]):
        out_ref[target, :, :length] = ordered_ref[target]
        out_ref[target, :, length:] = table


def pool(both_ref, out_ref):
    length = out_ref.shape[0]
    out_ref[...] = matmul_tn(both_ref[:, :length], both_ref[:, length:]).astype(BF16)


def per_sample(matrix, samples):
    few, tables = matrix.shape
    rows, columns = few * samples, samples * tables
    tall = ones_where(number((rows, few), 0) // samples == number((rows, few), 1))
    wide = ones_where(number((tables, columns), 1) % tables == number((tables, columns), 0))
    values = matmul(matmul(tall, matrix).astype(BF16), wide)
    own = number((rows, columns), 0) % samples == number((rows, columns), 1) // tables
    return jnp.where(own, values, 0.0).astype(BF16)


def norm_rows(values, gain):
    mean = jnp.mean(values, axis=-1, keepdims=True)
    centered = values - mean
    spread_ = jnp.mean(centered * centered, axis=-1, keepdims=True)
    return centered * lax.rsqrt(spread_ + 1e-05) * gain


def gain_blocks(gain, rank):
    flat = gain.shape[1]
    tables = flat // rank
    lane = number((16, flat), 1)
    own = lane % rank == number((16, flat), 0)
    to_table = ones_where(
        number((flat, LANES), 0) // rank == number((flat, LANES), 1) % tables
    )
    total = jnp.zeros((16, LANES), F32)
    for _ in range(3):
        part = gain.astype(BF16).astype(F32)
        gain = gain - part
        total = total + matmul(jnp.where(own, part, 0.0).astype(BF16), to_table)
    first = number((1, LANES), 1) < tables
    return [
        jnp.where(first, total[k : k + 1], total[k + 1 : k + 2]) for k in range(0, rank, 2)
    ]


def interactions(state, proj_ref, gain_ref, layer, flat_ref):
    rows = state.shape[0]
    samples = flat_ref.shape[1]
    rank, _, tables = proj_ref.shape
    proj = jnp.concatenate(
        [proj_ref[...].astype(F32)[:, layer, :], jnp.zeros((16 - rank, tables), F32)], axis=0
    ).astype(BF16)
    proj = per_sample(proj, samples)[: rank * samples]
    gain = jnp.concatenate(gain_blocks(gain_ref[layer : layer + 1, :], rank), axis=1)
    inner = matmul(proj, state).astype(BF16)
    inter = matmul_nt(inner, state)
    own = number(inter.shape, 0) % samples == number(inter.shape, 1) // tables
    inter = jnp.where(own, inter, 0.0)
    while inter.shape[1] > LANES:
        half = inter.shape[1] // 2
        inter = inter[:, :half] + inter[:, half:]
    inter = inter + pltpu.roll(inter, tables, 1)
    first = number((samples, LANES), 1) < tables
    flat = jnp.concatenate(
        [
            jnp.where(first, inter[at : at + samples], inter[at + samples : at + 2 * samples])
            for at in range(0, inter.shape[0], 2 * samples)
        ],
        axis=1,
    )
    flat = norm_rows(flat, gain).astype(BF16)
    for target in range(flat_ref.shape[0]):
        flat_ref[target] = flat


def first_layer(
    weight_hbm, moved_ref, host_ref, proj_ref, gain_ref, state_ref, flat_ref, weight_ref, sems
):
    copies = fetch([(weight_hbm.at[0], weight_ref.at[0])], sems)
    rows = state_ref.shape[0]
    tables = host_ref.shape[1]
    samples = rows // tables
    holder = ones_where(number((tables, tables), 0) == host_ref[...])
    tall = ones_where(number((rows, tables), 0) % tables == number((rows, tables), 1))
    wide = ones_where(number((tables, rows), 1) // samples == number((tables, rows), 0))
    place = matmul(matmul_nt(tall, holder).astype(BF16), wide)
    own = number((rows, rows), 0) // tables == number((rows, rows), 1) % samples
    place = jnp.where(own, place, 0.0).astype(BF16)
    state = matmul(place, moved_ref[...]).astype(BF16)
    state_ref[...] = state
    interactions(state, proj_ref, gain_ref, 0, flat_ref)
    copies[0].wait()


def map_columns(layer, rank, flat_ref, weight_ref, out_ref):
    flat = flat_ref.shape[1]
    tables = flat // rank
    row = number((flat, flat), 0)
    order = ones_where((row % tables) * rank + row // tables == number((flat, flat), 1))
    out_ref[...] = matmul(
        matmul(flat_ref[...], order).astype(BF16), weight_ref[min(layer, weight_ref.shape[0] - 1)]
    ).astype(BF16)


def next_state(layer, mixed_ref, state_ref, lin_ref, scale_ref):
    rows, width = state_ref.shape
    sources, samples, part = mixed_ref.shape
    made = sources * part // width
    tables = rows // samples
    mixed = jnp.concatenate(
        [
            mixed_ref[source, :, start : start + width].astype(F32)
            for source in range(sources)
            for start in range(0, part, width)
        ],
        axis=0,
    ).astype(BF16)
    row = number((made * samples, made * samples), 0)
    turn = ones_where(
        (row % made) * samples + row // made == number((made * samples, made * samples), 1)
    )
    mixed = matmul(turn, mixed)
    joined = []
    for sample in range(samples):
        joined.append(mixed[sample * made : (sample + 1) * made])
        joined.append(
            matmul(lin_ref[layer], state_ref[sample * tables : (sample + 1) * tables, :])
        )
    joined = jnp.concatenate(joined, axis=0) + state_ref[...].astype(F32)
    return norm_rows(joined, scale_ref[layer : layer + 1, :]).astype(BF16)


def next_layer(
    layer, mixed_ref, old_ref, lin_ref, scale_ref, proj_ref, gain_ref, state_ref, flat_ref
):
    state = next_state(layer, mixed_ref, old_ref, lin_ref, scale_ref)
    state_ref[...] = state
    interactions(state, proj_ref, gain_ref, layer + 1, flat_ref)


def last_state(layer, mixed_ref, old_ref, lin_ref, scale_ref, out_ref):
    out_ref[...] = next_state(layer, mixed_ref, old_ref, lin_ref, scale_ref)


def call(kernel, out_shape, *args, own=(), scratch=(), flops=0, limit=SMALL):
    moved = sum(a.size * a.dtype.itemsize for a in (*own, *args))
    return pl.pallas_call(
        kernel,
        out_shape=out_shape,
        in_specs=[pl.BlockSpec(memory_space=pl.ANY)] * len(own)
        + [pl.BlockSpec(memory_space=pltpu.VMEM)] * len(args),
        out_specs=jax.tree.map(lambda _: pl.BlockSpec(memory_space=pltpu.VMEM), out_shape),
        scratch_shapes=list(scratch),
        compiler_params=pltpu.CompilerParams(vmem_limit_bytes=limit),
        cost_estimate=pl.CostEstimate(flops=flops, bytes_accessed=moved, transcendentals=0),
    )(*own, *args)


def exchange(value, axis):
    return lax.all_to_all(value, axis, 0, 0, tiled=False)


def shards(
    checkpoint,
    counts,
    table_host,
    stored_slot,
    owner_order,
    fm_proj,
    fm_weight,
    fm_gain,
    lin_weight,
    out_gain,
):
    hosts = lax.axis_size("hst")
    locals_ = lax.axis_size("local")
    width = checkpoint.shape[-1]
    tables = table_host.shape[0]
    batch = owner_order.shape[0]
    samples = batch // (hosts * locals_)
    rows = counts.shape[2]
    length = hosts * samples
    state_rows = tables * samples
    rank = fm_proj.shape[2]
    flat_size = tables * rank

    def shape(dims, dtype=BF16):
        return jax.ShapeDtypeStruct(dims, dtype)

    def fetched(*arrays):
        return [pltpu.VMEM(a.shape, a.dtype) for a in arrays]

    host = table_host.reshape(1, tables)
    picked = (host, stored_slot.reshape(1, tables), checkpoint.reshape(tables, width))
    outgoing = call(
        pick_rows,
        shape((tables, 1, width), F32),
        own=picked,
        scratch=[*fetched(*picked), pltpu.SemaphoreType.DMA((3,))],
        limit=LARGE,
    )
    arrived = exchange(outgoing, "hst")
    ordered = call(
        order_counts,
        shape((locals_, rows, length)),
        jnp.transpose(counts[0]),
        owner_order.reshape(batch // LANES, LANES),

        scratch=[pltpu.VMEM((batch // LOW * (rows // PACK), LOW), BF16)],
        flops=2 * batch * (LOW * LOW + 64 * LANES),
    )
    both = exchange(
        call(join_table, shape((locals_, rows, length + width)), arrived, ordered), "local"
    )
    pooled = call(pool, shape((length, width)), both.reshape(locals_ * rows, length + width))
    moved = exchange(pooled.reshape(hosts, samples, width), "hst")

    made = (
        shape((state_rows, width)),
        shape((locals_, samples, flat_size)),
    )
    proj = jnp.transpose(fm_proj, (2, 0, 1))
    state, flat, weight = call(
        first_layer,
        (*made, shape((1, *fm_weight.shape[1:]))),
        moved.reshape(state_rows, width),
        host,
        proj,
        fm_gain,
        own=(fm_weight,),
        scratch=[pltpu.SemaphoreType.DMA((1,))],
        limit=MIDDLE,
    )
    for layer in range(LAYERS):
        gathered = exchange(flat, "local").reshape(locals_ * samples, flat_size)
        columns = call(
            lambda *refs, layer=layer: map_columns(layer, rank, *refs),
            shape((locals_ * samples, fm_weight.shape[2])),
            gathered,
            fm_weight if layer else weight,
        )
        mixed = exchange(columns.reshape(locals_, samples, -1), "local")
        if layer + 1 < LAYERS:
            state, flat = call(
                lambda *refs, layer=layer: next_layer(layer, *refs),
                made,
                mixed,
                state,
                lin_weight,
                out_gain,
                proj,
                fm_gain,
            )
        else:
            state = call(
                lambda *refs, layer=layer: last_state(layer, *refs),
                shape((state_rows, width)),
                mixed,
                state,
                lin_weight,
                out_gain,
            )
    return state.reshape(samples, tables, width)


def solution(mesh):
    placed = (
        P(None, "local", "hst", None),
        P("hst", None, "local"),
        P(),
        P(),
        P(),
        P(),
        P(None, None, "local"),
        P(),
        P(),
        P(),
    )
    return jax.shard_map(
        shards,
        mesh=mesh,
        in_specs=placed,
        out_specs=P(("hst", "local"), None, None),
        check_vma=False,
    )
```

```python
import jax
import jax.numpy as jnp
from jax import lax
from jax.experimental import pallas as pl
from jax.experimental.pallas import tpu as pltpu
from jax.sharding import PartitionSpec as P

LAYERS = 2
PACK = 4
LOW = 256
LANES = 128
SIDE = 8
FIRST, SECOND = (6, 4), (4, 4)
SMALL, MIDDLE, LARGE = 40 << 20, 49 << 20, 60 << 20
F32 = jnp.float32
BF16 = jnp.bfloat16


def number(shape, axis):
    return lax.broadcasted_iota(jnp.int32, shape, axis)


def ones_where(condition):
    return jnp.where(condition, 1.0, 0.0).astype(BF16)


def matmul(a, b):
    return jnp.dot(a, b, preferred_element_type=F32)


def matmul_nt(a, b):
    return lax.dot_general(a, b, (((1,), (1,)), ((), ())), preferred_element_type=F32)


def matmul_tn(a, b):
    return lax.dot_general(a, b, (((0,), (0,)), ((), ())), preferred_element_type=F32)


def fetch(pairs, sems):
    copies = [pltpu.make_async_copy(source, target, sems.at[at]) for at, (source, target) in enumerate(pairs)]
    for copy in copies:
        copy.start()
    return copies


def host_of(rank, start):
    return (rank // SIDE + start[0]) % SIDE * SIDE + (rank % SIDE + start[1]) % SIDE


def pick_rows(host_hbm, slot_hbm, stored_hbm, out_ref, host_ref, slot_ref, stored_ref, sems):
    for copy in fetch([(host_hbm, host_ref), (slot_hbm, slot_ref), (stored_hbm, stored_ref)], sems):
        copy.wait()
    tables = stored_ref.shape[0]
    holder = ones_where(host_of(number((tables, tables), 0), FIRST) == host_ref[...])
    slot = ones_where(number((tables, tables), 0) == slot_ref[...])
    chosen = matmul_nt(holder, slot).astype(BF16)
    out_ref[:, 0, :] = matmul(chosen, stored_ref[...])


def order_counts(counts_ref, order_ref, out_ref, packed_ref):
    rows, batch = counts_ref.shape
    targets, _, length = out_ref.shape
    words = rows // PACK
    high_count = batch // LOW
    order_rows = order_ref.shape[0]
    samples = 8
    word = counts_ref[0:words, :]
    for k in range(1, PACK):
        word = word + (counts_ref[k * words : (k + 1) * words, :] << (2 * k))
    word = word.astype(F32).astype(BF16)
    for high in range(high_count):
        packed_ref[high * words : (high + 1) * words, :] = word[:, high * LOW : (high + 1) * LOW]
    order = order_ref[...]
    parts = jnp.concatenate([order >> 8, order & (LOW - 1)], axis=0).astype(F32).astype(BF16)
    for target in range(targets):
        m = number((LANES, length), 1)
        row = host_of(m // samples, SECOND) * (targets * samples) + target * samples + m % samples
        found = matmul(parts, ones_where(number((LANES, length), 0) == row % LANES))
        m = number((2 * order_rows, length), 1)
        row = host_of(m // samples, SECOND) * (targets * samples) + target * samples + m % samples
        found = jnp.where(
            number((2 * order_rows, length), 0) % order_rows == row // LANES, found, 0.0
        )
        high_part = jnp.sum(found[:order_rows], axis=0, keepdims=True).astype(jnp.int32)
        low_part = jnp.sum(found[order_rows:], axis=0, keepdims=True).astype(jnp.int32)
        picked = matmul(packed_ref[...], ones_where(number((LOW, length), 0) == low_part))
        value = jnp.zeros((words, length), F32)
        for high in range(high_count):
            value = value + jnp.where(
                high_part == high, picked[high * words : (high + 1) * words, :], 0.0
            )
        value = value.astype(jnp.int32)
        for k in range(PACK):
            out_ref[target, k * words : (k + 1) * words, :] = (
                ((value >> (2 * k)) & 3).astype(F32).astype(BF16)
            )


def join_table(arrived_ref, ordered_ref, out_ref):
    length = ordered_ref.shape[2]
    rows = arrived_ref.shape[0]
    place = ones_where(number((rows, rows), 0) == host_of(number((rows, rows), 1), FIRST))
    table = matmul(place, arrived_ref[:, 0, :].astype(BF16)).astype(BF16)
    for target in range(out_ref.shape[0]):
        out_ref[target, :, :length] = ordered_ref[target]
        out_ref[target, :, length:] = table


def pool(both_ref, out_ref):
    length = out_ref.shape[0]
    out_ref[...] = matmul_tn(both_ref[:, :length], both_ref[:, length:]).astype(BF16)


def per_sample(matrix, samples):
    few, tables = matrix.shape
    rows, columns = few * samples, samples * tables
    tall = ones_where(number((rows, few), 0) // samples == number((rows, few), 1))
    wide = ones_where(number((tables, columns), 1) % tables == number((tables, columns), 0))
    values = matmul(matmul(tall, matrix).astype(BF16), wide)
    own = number((rows, columns), 0) % samples == number((rows, columns), 1) // tables
    return jnp.where(own, values, 0.0).astype(BF16)


def norm_rows(values, gain):
    mean = jnp.mean(values, axis=-1, keepdims=True)
    centered = values - mean
    spread_ = jnp.mean(centered * centered, axis=-1, keepdims=True)
    return centered * lax.rsqrt(spread_ + 1e-05) * gain


def gain_blocks(gain, rank):
    flat = gain.shape[1]
    tables = flat // rank
    lane = number((16, flat), 1)
    own = lane % rank == number((16, flat), 0)
    to_table = ones_where(
        number((flat, LANES), 0) // rank == number((flat, LANES), 1) % tables
    )
    total = jnp.zeros((16, LANES), F32)
    for _ in range(3):
        part = gain.astype(BF16).astype(F32)
        gain = gain - part
        total = total + matmul(jnp.where(own, part, 0.0).astype(BF16), to_table)
    first = number((1, LANES), 1) < tables
    return [
        jnp.where(first, total[k : k + 1], total[k + 1 : k + 2]) for k in range(0, rank, 2)
    ]


def interactions(state, proj_ref, gain_ref, layer, flat_ref):
    rows = state.shape[0]
    samples = flat_ref.shape[1]
    rank, _, tables = proj_ref.shape
    proj = jnp.concatenate(
        [proj_ref[...].astype(F32)[:, layer, :], jnp.zeros((16 - rank, tables), F32)], axis=0
    ).astype(BF16)
    proj = per_sample(proj, samples)[: rank * samples]
    gain = jnp.concatenate(gain_blocks(gain_ref[layer : layer + 1, :], rank), axis=1)
    inner = matmul(proj, state).astype(BF16)
    inter = matmul_nt(inner, state)
    own = number(inter.shape, 0) % samples == number(inter.shape, 1) // tables
    inter = jnp.where(own, inter, 0.0)
    while inter.shape[1] > LANES:
        half = inter.shape[1] // 2
        inter = inter[:, :half] + inter[:, half:]
    inter = inter + pltpu.roll(inter, tables, 1)
    first = number((samples, LANES), 1) < tables
    flat = jnp.concatenate(
        [
            jnp.where(first, inter[at : at + samples], inter[at + samples : at + 2 * samples])
            for at in range(0, inter.shape[0], 2 * samples)
        ],
        axis=1,
    )
    flat = norm_rows(flat, gain).astype(BF16)
    for target in range(flat_ref.shape[0]):
        flat_ref[target] = flat


def first_layer(
    weight_hbm, moved_ref, host_ref, proj_ref, gain_ref, state_ref, flat_ref, weight_ref, sems
):
    copies = fetch([(weight_hbm.at[0], weight_ref.at[0])], sems)
    rows = state_ref.shape[0]
    tables = host_ref.shape[1]
    samples = rows // tables
    holder = ones_where(host_of(number((tables, tables), 0), SECOND) == host_ref[...])
    tall = ones_where(number((rows, tables), 0) % tables == number((rows, tables), 1))
    wide = ones_where(number((tables, rows), 1) // samples == number((tables, rows), 0))
    place = matmul(matmul_nt(tall, holder).astype(BF16), wide)
    own = number((rows, rows), 0) // tables == number((rows, rows), 1) % samples
    place = jnp.where(own, place, 0.0).astype(BF16)
    state = matmul(place, moved_ref[...]).astype(BF16)
    state_ref[...] = state
    interactions(state, proj_ref, gain_ref, 0, flat_ref)
    copies[0].wait()


def map_columns(layer, rank, flat_ref, weight_ref, out_ref):
    flat = flat_ref.shape[1]
    tables = flat // rank
    row = number((flat, flat), 0)
    order = ones_where((row % tables) * rank + row // tables == number((flat, flat), 1))
    out_ref[...] = matmul(
        matmul(flat_ref[...], order).astype(BF16), weight_ref[min(layer, weight_ref.shape[0] - 1)]
    ).astype(BF16)


def next_state(layer, mixed_ref, state_ref, lin_ref, scale_ref):
    rows, width = state_ref.shape
    sources, samples, part = mixed_ref.shape
    made = sources * part // width
    tables = rows // samples
    mixed = jnp.concatenate(
        [
            mixed_ref[source, :, start : start + width].astype(F32)
            for source in range(sources)
            for start in range(0, part, width)
        ],
        axis=0,
    ).astype(BF16)
    row = number((made * samples, made * samples), 0)
    turn = ones_where(
        (row % made) * samples + row // made == number((made * samples, made * samples), 1)
    )
    mixed = matmul(turn, mixed)
    joined = []
    for sample in range(samples):
        joined.append(mixed[sample * made : (sample + 1) * made])
        joined.append(
            matmul(lin_ref[layer], state_ref[sample * tables : (sample + 1) * tables, :])
        )
    joined = jnp.concatenate(joined, axis=0) + state_ref[...].astype(F32)
    return norm_rows(joined, scale_ref[layer : layer + 1, :]).astype(BF16)


def next_layer(
    layer, mixed_ref, old_ref, lin_ref, scale_ref, proj_ref, gain_ref, state_ref, flat_ref
):
    state = next_state(layer, mixed_ref, old_ref, lin_ref, scale_ref)
    state_ref[...] = state
    interactions(state, proj_ref, gain_ref, layer + 1, flat_ref)


def last_state(layer, mixed_ref, old_ref, lin_ref, scale_ref, out_ref):
    out_ref[...] = next_state(layer, mixed_ref, old_ref, lin_ref, scale_ref)


def call(kernel, out_shape, *args, own=(), scratch=(), flops=0, limit=SMALL):
    moved = sum(a.size * a.dtype.itemsize for a in (*own, *args))
    return pl.pallas_call(
        kernel,
        out_shape=out_shape,
        in_specs=[pl.BlockSpec(memory_space=pl.ANY)] * len(own)
        + [pl.BlockSpec(memory_space=pltpu.VMEM)] * len(args),
        out_specs=jax.tree.map(lambda _: pl.BlockSpec(memory_space=pltpu.VMEM), out_shape),
        scratch_shapes=list(scratch),
        compiler_params=pltpu.CompilerParams(vmem_limit_bytes=limit),
        cost_estimate=pl.CostEstimate(flops=flops, bytes_accessed=moved, transcendentals=0),
    )(*own, *args)


def exchange(value, axis, groups=None):
    return lax.all_to_all(value, axis, 0, 0, tiled=False, axis_index_groups=groups)


def shards(
    checkpoint,
    counts,
    table_host,
    stored_slot,
    owner_order,
    fm_proj,
    fm_weight,
    fm_gain,
    lin_weight,
    out_gain,
):
    hosts = lax.axis_size("hst")
    locals_ = lax.axis_size("local")
    width = checkpoint.shape[-1]
    tables = table_host.shape[0]
    batch = owner_order.shape[0]
    samples = batch // (hosts * locals_)
    rows = counts.shape[2]
    length = hosts * samples
    state_rows = tables * samples
    rank = fm_proj.shape[2]
    flat_size = tables * rank

    def shape(dims, dtype=BF16):
        return jax.ShapeDtypeStruct(dims, dtype)

    def fetched(*arrays):
        return [pltpu.VMEM(a.shape, a.dtype) for a in arrays]

    host = table_host.reshape(1, tables)
    picked = (host, stored_slot.reshape(1, tables), checkpoint.reshape(tables, width))
    outgoing = call(
        pick_rows,
        shape((tables, 1, width), F32),
        own=picked,
        scratch=[*fetched(*picked), pltpu.SemaphoreType.DMA((3,))],
        limit=LARGE,
    )
    arrived = exchange(outgoing, "hst", [[host_of(rank, FIRST) for rank in range(hosts)]])
    ordered = call(
        order_counts,
        shape((locals_, rows, length)),
        jnp.transpose(counts[0]),
        owner_order.reshape(batch // LANES, LANES),

        scratch=[pltpu.VMEM((batch // LOW * (rows // PACK), LOW), BF16)],
        flops=2 * batch * (LOW * LOW + 64 * LANES),
    )
    both = exchange(
        call(join_table, shape((locals_, rows, length + width)), arrived, ordered), "local"
    )
    pooled = call(pool, shape((length, width)), both.reshape(locals_ * rows, length + width))
    moved = exchange(
        pooled.reshape(hosts, samples, width),
        "hst",
        [[host_of(rank, SECOND) for rank in range(hosts)]],
    )

    made = (
        shape((state_rows, width)),
        shape((locals_, samples, flat_size)),
    )
    proj = jnp.transpose(fm_proj, (2, 0, 1))
    state, flat, weight = call(
        first_layer,
        (*made, shape((1, *fm_weight.shape[1:]))),
        moved.reshape(state_rows, width),
        host,
        proj,
        fm_gain,
        own=(fm_weight,),
        scratch=[pltpu.SemaphoreType.DMA((1,))],
        limit=MIDDLE,
    )
    for layer in range(LAYERS):
        gathered = exchange(flat, "local").reshape(locals_ * samples, flat_size)
        columns = call(
            lambda *refs, layer=layer: map_columns(layer, rank, *refs),
            shape((locals_ * samples, fm_weight.shape[2])),
            gathered,
            fm_weight if layer else weight,
        )
        mixed = exchange(columns.reshape(locals_, samples, -1), "local")
        if layer + 1 < LAYERS:
            state, flat = call(
                lambda *refs, layer=layer: next_layer(layer, *refs),
                made,
                mixed,
                state,
                lin_weight,
                out_gain,
                proj,
                fm_gain,
            )
        else:
            state = call(
                lambda *refs, layer=layer: last_state(layer, *refs),
                shape((state_rows, width)),
                mixed,
                state,
                lin_weight,
                out_gain,
            )
    return state.reshape(samples, tables, width)


def solution(mesh):
    placed = (
        P(None, "local", "hst", None),
        P("hst", None, "local"),
        P(),
        P(),
        P(),
        P(),
        P(None, None, "local"),
        P(),
        P(),
        P(),
    )
    return jax.shard_map(
        shards,
        mesh=mesh,
        in_specs=placed,
        out_specs=P(("hst", "local"), None, None),
        check_vma=False,
    )
```

```python
import jax
import jax.numpy as jnp
from jax import lax
from jax.experimental import pallas as pl
from jax.experimental.pallas import tpu as pltpu
from jax.sharding import PartitionSpec as P

LAYERS = 2
PACK = 4
LOW = 256
LANES = 128
NEAR, LAST = 5, 5
SIDE = 8
FIRST, SECOND = (6, 4), (4, 4)
SMALL, MIDDLE, LARGE = 40 << 20, 49 << 20, 60 << 20
F32 = jnp.float32
BF16 = jnp.bfloat16


def number(shape, axis):
    return lax.broadcasted_iota(jnp.int32, shape, axis)


def ones_where(condition):
    return jnp.where(condition, 1.0, 0.0).astype(BF16)


def matmul(a, b):
    return jnp.dot(a, b, preferred_element_type=F32)


def matmul_nt(a, b):
    return lax.dot_general(a, b, (((1,), (1,)), ((), ())), preferred_element_type=F32)


def matmul_tn(a, b):
    return lax.dot_general(a, b, (((0,), (0,)), ((), ())), preferred_element_type=F32)


def fetch(pairs, sems):
    copies = [pltpu.make_async_copy(source, target, sems.at[at]) for at, (source, target) in enumerate(pairs)]
    for copy in copies:
        copy.start()
    return copies


def local_of(rank, start):
    return (rank + start) % 8


def host_of(rank, start):
    return (rank // SIDE + start[0]) % SIDE * SIDE + (rank % SIDE + start[1]) % SIDE


def pick_rows(host_hbm, slot_hbm, stored_hbm, out_ref, host_ref, slot_ref, stored_ref, sems):
    for copy in fetch([(host_hbm, host_ref), (slot_hbm, slot_ref), (stored_hbm, stored_ref)], sems):
        copy.wait()
    tables = stored_ref.shape[0]
    holder = ones_where(host_of(number((tables, tables), 0), FIRST) == host_ref[...])
    slot = ones_where(number((tables, tables), 0) == slot_ref[...])
    chosen = matmul_nt(holder, slot).astype(BF16)
    out_ref[:, 0, :] = matmul(chosen, stored_ref[...])


def order_counts(counts_ref, order_ref, out_ref, packed_ref):
    rows, batch = counts_ref.shape
    targets, _, length = out_ref.shape
    words = rows // PACK
    high_count = batch // LOW
    order_rows = order_ref.shape[0]
    samples = 8
    word = counts_ref[0:words, :]
    for k in range(1, PACK):
        word = word + (counts_ref[k * words : (k + 1) * words, :] << (2 * k))
    word = word.astype(F32).astype(BF16)
    for high in range(high_count):
        packed_ref[high * words : (high + 1) * words, :] = word[:, high * LOW : (high + 1) * LOW]
    order = order_ref[...]
    parts = jnp.concatenate([order >> 8, order & (LOW - 1)], axis=0).astype(F32).astype(BF16)
    for target in range(targets):
        m = number((1, length), 1)
        row = host_of(m // samples, SECOND) * (targets * samples) + local_of(target, NEAR) * samples + m % samples
        found = matmul(parts, ones_where(number((LANES, length), 0) == row % LANES))
        found = jnp.where(
            number((2 * order_rows, length), 0) % order_rows == row // LANES, found, 0.0
        )
        high_part = jnp.sum(found[:order_rows], axis=0, keepdims=True).astype(jnp.int32)
        low_part = jnp.sum(found[order_rows:], axis=0, keepdims=True).astype(jnp.int32)
        picked = matmul(packed_ref[...], ones_where(number((LOW, length), 0) == low_part))
        value = jnp.zeros((words, length), F32)
        for high in range(high_count):
            value = value + jnp.where(
                high_part == high, picked[high * words : (high + 1) * words, :], 0.0
            )
        value = value.astype(jnp.int32)
        for k in range(PACK):
            out_ref[target, k * words : (k + 1) * words, :] = (
                ((value >> (2 * k)) & 3).astype(F32).astype(BF16)
            )


def join_table(arrived_ref, ordered_ref, out_ref):
    length = ordered_ref.shape[2]
    rows = arrived_ref.shape[0]
    place = ones_where(number((rows, rows), 0) == host_of(number((rows, rows), 1), FIRST))
    table = matmul(place, arrived_ref[:, 0, :].astype(BF16)).astype(BF16)
    for target in range(out_ref.shape[0]):
        out_ref[target, :, :length] = ordered_ref[target]
        out_ref[target, :, length:] = table


def pool(both_ref, out_ref):
    length = out_ref.shape[0]
    out_ref[...] = matmul_tn(both_ref[:, :length], both_ref[:, length:]).astype(BF16)


def per_sample(matrix, samples):
    few, tables = matrix.shape
    rows, columns = few * samples, samples * tables
    tall = ones_where(number((rows, few), 0) // samples == number((rows, few), 1))
    wide = ones_where(number((tables, columns), 1) % tables == number((tables, columns), 0))
    values = matmul(matmul(tall, matrix).astype(BF16), wide)
    own = number((rows, columns), 0) % samples == number((rows, columns), 1) // tables
    return jnp.where(own, values, 0.0).astype(BF16)


def norm_rows(values, gain):
    mean = jnp.mean(values, axis=-1, keepdims=True)
    centered = values - mean
    spread_ = jnp.mean(centered * centered, axis=-1, keepdims=True)
    return centered * lax.rsqrt(spread_ + 1e-05) * gain


def gain_blocks(gain, rank):
    flat = gain.shape[1]
    tables = flat // rank
    lane = number((16, flat), 1)
    own = lane % rank == number((16, flat), 0)
    to_table = ones_where(
        number((flat, LANES), 0) // rank == number((flat, LANES), 1) % tables
    )
    total = jnp.zeros((16, LANES), F32)
    for _ in range(3):
        part = gain.astype(BF16).astype(F32)
        gain = gain - part
        total = total + matmul(jnp.where(own, part, 0.0).astype(BF16), to_table)
    first = number((1, LANES), 1) < tables
    return [
        jnp.where(first, total[k : k + 1], total[k + 1 : k + 2]) for k in range(0, rank, 2)
    ]


def interactions(state, proj_ref, gain_ref, layer, flat_ref):
    rows = state.shape[0]
    samples = flat_ref.shape[1]
    rank, _, tables = proj_ref.shape
    proj = jnp.concatenate(
        [proj_ref[...].astype(F32)[:, layer, :], jnp.zeros((16 - rank, tables), F32)], axis=0
    ).astype(BF16)
    proj = per_sample(proj, samples)[: rank * samples]
    gain = jnp.concatenate(gain_blocks(gain_ref[layer : layer + 1, :], rank), axis=1)
    inner = matmul(proj, state).astype(BF16)
    inter = matmul_nt(inner, state)
    own = number(inter.shape, 0) % samples == number(inter.shape, 1) // tables
    inter = jnp.where(own, inter, 0.0)
    while inter.shape[1] > LANES:
        half = inter.shape[1] // 2
        inter = inter[:, :half] + inter[:, half:]
    inter = inter + pltpu.roll(inter, tables, 1)
    first = number((samples, LANES), 1) < tables
    flat = jnp.concatenate(
        [
            jnp.where(first, inter[at : at + samples], inter[at + samples : at + 2 * samples])
            for at in range(0, inter.shape[0], 2 * samples)
        ],
        axis=1,
    )
    flat = norm_rows(flat, gain).astype(BF16)
    for target in range(flat_ref.shape[0]):
        flat_ref[target] = flat


def first_layer(
    weight_hbm, moved_ref, host_ref, proj_ref, gain_ref, state_ref, flat_ref, weight_ref, sems
):
    copies = fetch([(weight_hbm.at[0], weight_ref.at[0])], sems)
    rows = state_ref.shape[0]
    tables = host_ref.shape[1]
    samples = rows // tables
    holder = ones_where(host_of(number((tables, tables), 0), SECOND) == host_ref[...])
    tall = ones_where(number((rows, tables), 0) % tables == number((rows, tables), 1))
    wide = ones_where(number((tables, rows), 1) // samples == number((tables, rows), 0))
    place = matmul(matmul_nt(tall, holder).astype(BF16), wide)
    own = number((rows, rows), 0) // tables == number((rows, rows), 1) % samples
    place = jnp.where(own, place, 0.0).astype(BF16)
    state = matmul(place, moved_ref[...]).astype(BF16)
    state_ref[...] = state
    interactions(state, proj_ref, gain_ref, 0, flat_ref)
    copies[0].wait()


def map_columns(layer, rank, flat_ref, weight_ref, out_ref):
    flat = flat_ref.shape[1]
    tables = flat // rank
    row = number((flat, flat), 0)
    order = ones_where((row % tables) * rank + row // tables == number((flat, flat), 1))
    out_ref[...] = matmul(
        matmul(flat_ref[...], order).astype(BF16), weight_ref[min(layer, weight_ref.shape[0] - 1)]
    ).astype(BF16)


def next_state(layer, mixed_ref, state_ref, lin_ref, scale_ref):
    rows, width = state_ref.shape
    sources, samples, part = mixed_ref.shape
    made = sources * part // width
    tables = rows // samples
    mixed = jnp.concatenate(
        [
            mixed_ref[(source - LAST) % sources, :, start : start + width].astype(F32)
            for source in range(sources)
            for start in range(0, part, width)
        ],
        axis=0,
    ).astype(BF16)
    row = number((made * samples, made * samples), 0)
    turn = ones_where(
        (row % made) * samples + row // made == number((made * samples, made * samples), 1)
    )
    mixed = matmul(turn, mixed)
    joined = []
    for sample in range(samples):
        joined.append(mixed[sample * made : (sample + 1) * made])
        joined.append(
            matmul(lin_ref[layer], state_ref[sample * tables : (sample + 1) * tables, :])
        )
    joined = jnp.concatenate(joined, axis=0) + state_ref[...].astype(F32)
    return norm_rows(joined, scale_ref[layer : layer + 1, :]).astype(BF16)


def next_layer(
    layer, mixed_ref, old_ref, lin_ref, scale_ref, proj_ref, gain_ref, state_ref, flat_ref
):
    state = next_state(layer, mixed_ref, old_ref, lin_ref, scale_ref)
    state_ref[...] = state
    interactions(state, proj_ref, gain_ref, layer + 1, flat_ref)


def last_state(layer, mixed_ref, old_ref, lin_ref, scale_ref, out_ref):
    out_ref[...] = next_state(layer, mixed_ref, old_ref, lin_ref, scale_ref)


def call(kernel, out_shape, *args, own=(), scratch=(), flops=0, limit=SMALL):
    moved = sum(a.size * a.dtype.itemsize for a in (*own, *args))
    return pl.pallas_call(
        kernel,
        out_shape=out_shape,
        in_specs=[pl.BlockSpec(memory_space=pl.ANY)] * len(own)
        + [pl.BlockSpec(memory_space=pltpu.VMEM)] * len(args),
        out_specs=jax.tree.map(lambda _: pl.BlockSpec(memory_space=pltpu.VMEM), out_shape),
        scratch_shapes=list(scratch),
        compiler_params=pltpu.CompilerParams(vmem_limit_bytes=limit),
        cost_estimate=pl.CostEstimate(flops=flops, bytes_accessed=moved, transcendentals=0),
    )(*own, *args)


def exchange(value, axis, groups=None):
    return lax.all_to_all(value, axis, 0, 0, tiled=False, axis_index_groups=groups)


def shards(
    checkpoint,
    counts,
    table_host,
    stored_slot,
    owner_order,
    fm_proj,
    fm_weight,
    fm_gain,
    lin_weight,
    out_gain,
):
    hosts = lax.axis_size("hst")
    locals_ = lax.axis_size("local")
    width = checkpoint.shape[-1]
    tables = table_host.shape[0]
    batch = owner_order.shape[0]
    samples = batch // (hosts * locals_)
    rows = counts.shape[2]
    length = hosts * samples
    state_rows = tables * samples
    rank = fm_proj.shape[2]
    flat_size = tables * rank

    def shape(dims, dtype=BF16):
        return jax.ShapeDtypeStruct(dims, dtype)

    def fetched(*arrays):
        return [pltpu.VMEM(a.shape, a.dtype) for a in arrays]

    host = table_host.reshape(1, tables)
    picked = (host, stored_slot.reshape(1, tables), checkpoint.reshape(tables, width))
    outgoing = call(
        pick_rows,
        shape((tables, 1, width), F32),
        own=picked,
        scratch=[*fetched(*picked), pltpu.SemaphoreType.DMA((3,))],
        limit=LARGE,
    )
    arrived = exchange(outgoing, "hst", [[host_of(rank, FIRST) for rank in range(hosts)]])
    ordered = call(
        order_counts,
        shape((locals_, rows, length)),
        jnp.transpose(counts[0]),
        owner_order.reshape(batch // LANES, LANES),

        scratch=[pltpu.VMEM((batch // LOW * (rows // PACK), LOW), BF16)],
        flops=2 * batch * (LOW * LOW + 64 * LANES),
    )
    both = exchange(
        call(join_table, shape((locals_, rows, length + width)), arrived, ordered),
        "local",
        [[local_of(rank, NEAR) for rank in range(locals_)]],
    )
    pooled = call(pool, shape((length, width)), both.reshape(locals_ * rows, length + width))
    moved = exchange(
        pooled.reshape(hosts, samples, width),
        "hst",
        [[host_of(rank, SECOND) for rank in range(hosts)]],
    )

    made = (
        shape((state_rows, width)),
        shape((locals_, samples, flat_size)),
    )
    proj = jnp.transpose(fm_proj, (2, 0, 1))
    state, flat, weight = call(
        first_layer,
        (*made, shape((1, *fm_weight.shape[1:]))),
        moved.reshape(state_rows, width),
        host,
        proj,
        fm_gain,
        own=(fm_weight,),
        scratch=[pltpu.SemaphoreType.DMA((1,))],
        limit=MIDDLE,
    )
    last = [[local_of(rank, LAST) for rank in range(locals_)]]
    for layer in range(LAYERS):
        gathered = exchange(flat, "local", last).reshape(locals_ * samples, flat_size)
        columns = call(
            lambda *refs, layer=layer: map_columns(layer, rank, *refs),
            shape((locals_ * samples, fm_weight.shape[2])),
            gathered,
            fm_weight if layer else weight,
        )
        mixed = exchange(columns.reshape(locals_, samples, -1), "local", last)
        if layer + 1 < LAYERS:
            state, flat = call(
                lambda *refs, layer=layer: next_layer(layer, *refs),
                made,
                mixed,
                state,
                lin_weight,
                out_gain,
                proj,
                fm_gain,
            )
        else:
            state = call(
                lambda *refs, layer=layer: last_state(layer, *refs),
                shape((state_rows, width)),
                mixed,
                state,
                lin_weight,
                out_gain,
            )
    return state.reshape(samples, tables, width)


def solution(mesh):
    placed = (
        P(None, "local", "hst", None),
        P("hst", None, "local"),
        P(),
        P(),
        P(),
        P(),
        P(None, None, "local"),
        P(),
        P(),
        P(),
    )
    return jax.shard_map(
        shards,
        mesh=mesh,
        in_specs=placed,
        out_specs=P(("hst", "local"), None, None),
        check_vma=False,
    )
```

```python
import jax
import jax.numpy as jnp
from jax import lax
from jax.experimental import pallas as pl
from jax.experimental.pallas import tpu as pltpu
from jax.sharding import PartitionSpec as P

LAYERS = 2
PACK = 4
LOW = 256
LANES = 128
NEAR, LAST = 5, 5
SIDE = 8
FIRST, SECOND = (6, 4), (4, 4)
SMALL, MIDDLE, MORE, LARGE = 40 << 20, 49 << 20, 53 << 20, 60 << 20
F32 = jnp.float32
BF16 = jnp.bfloat16


def number(shape, axis):
    return lax.broadcasted_iota(jnp.int32, shape, axis)


def ones_where(condition):
    return jnp.where(condition, 1.0, 0.0).astype(BF16)


def matmul(a, b):
    return jnp.dot(a, b, preferred_element_type=F32)


def matmul_nt(a, b):
    return lax.dot_general(a, b, (((1,), (1,)), ((), ())), preferred_element_type=F32)


def matmul_tn(a, b):
    return lax.dot_general(a, b, (((0,), (0,)), ((), ())), preferred_element_type=F32)


def fetch(pairs, sems):
    copies = [pltpu.make_async_copy(source, target, sems.at[at]) for at, (source, target) in enumerate(pairs)]
    for copy in copies:
        copy.start()
    return copies


def local_of(rank, start):
    return (rank + start) % 8


def host_of(rank, start):
    return (rank // SIDE + start[0]) % SIDE * SIDE + (rank % SIDE + start[1]) % SIDE


def pick_rows(host_hbm, slot_hbm, stored_hbm, out_ref, host_ref, slot_ref, stored_ref, sems):
    for copy in fetch([(host_hbm, host_ref), (slot_hbm, slot_ref), (stored_hbm, stored_ref)], sems):
        copy.wait()
    tables = stored_ref.shape[0]
    holder = ones_where(host_of(number((tables, tables), 0), FIRST) == host_ref[...])
    slot = ones_where(number((tables, tables), 0) == slot_ref[...])
    chosen = matmul_nt(holder, slot).astype(BF16)
    out_ref[:, 0, :] = matmul(chosen, stored_ref[...])


def order_counts(counts_hbm, order_ref, out_ref, packed_ref, counts_ref, sems):
    copies = fetch([(counts_hbm, counts_ref)], sems)
    rows, batch = counts_ref.shape
    targets, _, length = out_ref.shape
    words = rows // PACK
    high_count = batch // LOW
    order_rows = order_ref.shape[0]
    samples = 8
    order = order_ref[...]
    parts = jnp.concatenate([order >> 8, order & (LOW - 1)], axis=0).astype(F32).astype(BF16)
    places = []
    for target in range(targets):
        m = number((1, length), 1)
        row = host_of(m // samples, SECOND) * (targets * samples)
        row = row + local_of(target, NEAR) * samples + m % samples
        found = matmul(parts, ones_where(number((LANES, length), 0) == row % LANES))
        found = jnp.where(
            number((2 * order_rows, length), 0) % order_rows == row // LANES, found, 0.0
        )
        high_part = jnp.sum(found[:order_rows], axis=0, keepdims=True).astype(jnp.int32)
        low_part = jnp.sum(found[order_rows:], axis=0, keepdims=True).astype(jnp.int32)
        places.append((high_part, low_part))
    copies[0].wait()
    word = counts_ref[0:words, :]
    for k in range(1, PACK):
        word = word + (counts_ref[k * words : (k + 1) * words, :] << (2 * k))
    word = word.astype(F32).astype(BF16)
    for high in range(high_count):
        packed_ref[high * words : (high + 1) * words, :] = word[:, high * LOW : (high + 1) * LOW]
    for target, (high_part, low_part) in enumerate(places):
        picked = matmul(packed_ref[...], ones_where(number((LOW, length), 0) == low_part))
        value = jnp.zeros((words, length), F32)
        for high in range(high_count):
            value = value + jnp.where(
                high_part == high, picked[high * words : (high + 1) * words, :], 0.0
            )
        value = value.astype(jnp.int32)
        for k in range(PACK):
            out_ref[target, k * words : (k + 1) * words, :] = (
                ((value >> (2 * k)) & 3).astype(F32).astype(BF16)
            )


def join_table(arrived_ref, ordered_ref, out_ref):
    length = ordered_ref.shape[2]
    rows = arrived_ref.shape[0]
    place = ones_where(number((rows, rows), 0) == host_of(number((rows, rows), 1), FIRST))
    table = matmul(place, arrived_ref[:, 0, :].astype(BF16)).astype(BF16)
    for target in range(out_ref.shape[0]):
        out_ref[target, :, :length] = ordered_ref[target]
        out_ref[target, :, length:] = table


def pool(both_ref, out_ref):
    length = out_ref.shape[0]
    out_ref[...] = matmul_tn(both_ref[:, :length], both_ref[:, length:]).astype(BF16)


def per_sample(matrix, samples):
    few, tables = matrix.shape
    rows, columns = few * samples, samples * tables
    tall = ones_where(number((rows, few), 0) // samples == number((rows, few), 1))
    wide = ones_where(number((1, columns), 1) % tables == number((tables, columns), 0))
    values = matmul(matmul(tall, matrix).astype(BF16), wide)
    own = number((rows, columns), 0) % samples == number((1, columns), 1) // tables
    return jnp.where(own, values, 0.0).astype(BF16)


def norm_rows(values, gain):
    mean = jnp.mean(values, axis=-1, keepdims=True)
    centered = values - mean
    spread_ = jnp.mean(centered * centered, axis=-1, keepdims=True)
    return centered * lax.rsqrt(spread_ + 1e-05) * gain


def gain_blocks(gain, rank):
    flat = gain.shape[1]
    tables = flat // rank
    own = number((1, flat), 1) % rank == number((16, flat), 0)
    row = number((flat, LANES), 0)
    least = number((1, LANES), 1) % tables * rank
    to_table = ones_where((row >= least) & (row < least + rank))
    total = jnp.zeros((16, LANES), F32)
    for _ in range(3):
        part = gain.astype(BF16).astype(F32)
        gain = gain - part
        total = total + matmul(jnp.where(own, part, 0.0).astype(BF16), to_table)
    first = number((1, LANES), 1) < tables
    return [
        jnp.where(first, total[k : k + 1], total[k + 1 : k + 2]) for k in range(0, rank, 2)
    ]


def interactions(state, proj_ref, gain_ref, layer, flat_ref):
    rows = state.shape[0]
    samples = flat_ref.shape[1]
    rank, _, tables = proj_ref.shape
    proj = jnp.concatenate(
        [proj_ref[...].astype(F32)[:, layer, :], jnp.zeros((16 - rank, tables), F32)], axis=0
    ).astype(BF16)
    proj = per_sample(proj, samples)[: rank * samples]
    gain = jnp.concatenate(gain_blocks(gain_ref[layer : layer + 1, :], rank), axis=1)
    inner = matmul(proj, state).astype(BF16)
    inter = matmul_nt(inner, state)
    own = number(inter.shape, 0) % samples == number((1, rows), 1) // tables
    inter = jnp.where(own, inter, 0.0)
    while inter.shape[1] > LANES:
        half = inter.shape[1] // 2
        inter = inter[:, :half] + inter[:, half:]
    inter = inter + pltpu.roll(inter, tables, 1)
    first = number((samples, LANES), 1) < tables
    flat = jnp.concatenate(
        [
            jnp.where(first, inter[at : at + samples], inter[at + samples : at + 2 * samples])
            for at in range(0, inter.shape[0], 2 * samples)
        ],
        axis=1,
    )
    flat = norm_rows(flat, gain).astype(BF16)
    for target in range(flat_ref.shape[0]):
        flat_ref[target] = flat


def first_layer(
    weight_hbm, moved_ref, host_ref, proj_ref, gain_ref, state_ref, flat_ref, weight_ref, sems
):
    copies = fetch([(weight_hbm.at[0], weight_ref.at[0])], sems)
    rows = state_ref.shape[0]
    tables = host_ref.shape[1]
    samples = rows // tables
    holder = ones_where(host_of(number((tables, tables), 0), SECOND) == host_ref[...])
    tall = ones_where(number((rows, tables), 0) % tables == number((rows, tables), 1))
    wide = ones_where(number((1, rows), 1) // samples == number((tables, rows), 0))
    place = matmul(matmul_nt(tall, holder).astype(BF16), wide)
    own = number((rows, rows), 0) // tables == number((1, rows), 1) % samples
    place = jnp.where(own, place, 0.0).astype(BF16)
    state = matmul(place, moved_ref[...]).astype(BF16)
    state_ref[...] = state
    interactions(state, proj_ref, gain_ref, 0, flat_ref)
    copies[0].wait()


def map_columns(layer, rank, flat_ref, weight_ref, out_ref):
    flat = flat_ref.shape[1]
    tables = flat // rank
    column = number((1, flat), 1)
    order = ones_where(
        number((flat, flat), 0) == (column % rank) * tables + column // rank
    )
    out_ref[...] = matmul(
        matmul(flat_ref[...], order).astype(BF16), weight_ref[min(layer, weight_ref.shape[0] - 1)]
    ).astype(BF16)


def next_state(layer, mixed_ref, state_ref, lin_ref, scale_ref):
    rows, width = state_ref.shape
    sources, samples, part = mixed_ref.shape
    made = sources * part // width
    tables = rows // samples
    mixed = jnp.concatenate(
        [
            mixed_ref[(source - LAST) % sources, :, start : start + width].astype(F32)
            for source in range(sources)
            for start in range(0, part, width)
        ],
        axis=0,
    ).astype(BF16)
    column = number((1, made * samples), 1)
    turn = ones_where(
        number((made * samples, made * samples), 0)
        == (column % samples) * made + column // samples
    )
    mixed = matmul(turn, mixed)
    joined = []
    for sample in range(samples):
        joined.append(mixed[sample * made : (sample + 1) * made])
        joined.append(
            matmul(lin_ref[layer], state_ref[sample * tables : (sample + 1) * tables, :])
        )
    joined = jnp.concatenate(joined, axis=0) + state_ref[...].astype(F32)
    return norm_rows(joined, scale_ref[layer : layer + 1, :]).astype(BF16)


def next_layer(
    layer, mixed_ref, old_ref, lin_ref, scale_ref, proj_ref, gain_ref, state_ref, flat_ref
):
    state = next_state(layer, mixed_ref, old_ref, lin_ref, scale_ref)
    state_ref[...] = state
    interactions(state, proj_ref, gain_ref, layer + 1, flat_ref)


def last_state(layer, mixed_ref, old_ref, lin_ref, scale_ref, out_ref):
    out_ref[...] = next_state(layer, mixed_ref, old_ref, lin_ref, scale_ref)


def call(kernel, out_shape, *args, own=(), scratch=(), flops=0, limit=SMALL):
    moved = sum(a.size * a.dtype.itemsize for a in (*own, *args))
    return pl.pallas_call(
        kernel,
        out_shape=out_shape,
        in_specs=[pl.BlockSpec(memory_space=pl.ANY)] * len(own)
        + [pl.BlockSpec(memory_space=pltpu.VMEM)] * len(args),
        out_specs=jax.tree.map(lambda _: pl.BlockSpec(memory_space=pltpu.VMEM), out_shape),
        scratch_shapes=list(scratch),
        compiler_params=pltpu.CompilerParams(vmem_limit_bytes=limit),
        cost_estimate=pl.CostEstimate(flops=flops, bytes_accessed=moved, transcendentals=0),
    )(*own, *args)


def exchange(value, axis, groups=None):
    return lax.all_to_all(value, axis, 0, 0, tiled=False, axis_index_groups=groups)


def shards(
    checkpoint,
    counts,
    table_host,
    stored_slot,
    owner_order,
    fm_proj,
    fm_weight,
    fm_gain,
    lin_weight,
    out_gain,
):
    hosts = lax.axis_size("hst")
    locals_ = lax.axis_size("local")
    width = checkpoint.shape[-1]
    tables = table_host.shape[0]
    batch = owner_order.shape[0]
    samples = batch // (hosts * locals_)
    rows = counts.shape[2]
    length = hosts * samples
    state_rows = tables * samples
    rank = fm_proj.shape[2]
    flat_size = tables * rank

    def shape(dims, dtype=BF16):
        return jax.ShapeDtypeStruct(dims, dtype)

    def fetched(*arrays):
        return [pltpu.VMEM(a.shape, a.dtype) for a in arrays]

    host = table_host.reshape(1, tables)
    picked = (host, stored_slot.reshape(1, tables), checkpoint.reshape(tables, width))
    outgoing = call(
        pick_rows,
        shape((tables, 1, width), F32),
        own=picked,
        scratch=[*fetched(*picked), pltpu.SemaphoreType.DMA((3,))],
        limit=LARGE,
    )
    arrived = exchange(outgoing, "hst", [[host_of(rank, FIRST) for rank in range(hosts)]])
    by_row = jnp.transpose(counts[0])
    ordered = call(
        order_counts,
        shape((locals_, rows, length)),
        owner_order.reshape(batch // LANES, LANES),
        own=(by_row,),
        scratch=[
            pltpu.VMEM((batch // LOW * (rows // PACK), LOW), BF16),
            *fetched(by_row),
            pltpu.SemaphoreType.DMA((1,)),
        ],
        flops=2 * batch * (LOW * LOW + 64 * LANES),
        limit=MORE,
    )
    both = exchange(
        call(join_table, shape((locals_, rows, length + width)), arrived, ordered),
        "local",
        [[local_of(rank, NEAR) for rank in range(locals_)]],
    )
    pooled = call(pool, shape((length, width)), both.reshape(locals_ * rows, length + width))
    moved = exchange(
        pooled.reshape(hosts, samples, width),
        "hst",
        [[host_of(rank, SECOND) for rank in range(hosts)]],
    )

    made = (
        shape((state_rows, width)),
        shape((locals_, samples, flat_size)),
    )
    proj = jnp.transpose(fm_proj, (2, 0, 1))
    state, flat, weight = call(
        first_layer,
        (*made, shape((1, *fm_weight.shape[1:]))),
        moved.reshape(state_rows, width),
        host,
        proj,
        fm_gain,
        own=(fm_weight,),
        scratch=[pltpu.SemaphoreType.DMA((1,))],
        limit=MIDDLE,
    )
    last = [[local_of(rank, LAST) for rank in range(locals_)]]
    for layer in range(LAYERS):
        gathered = exchange(flat, "local", last).reshape(locals_ * samples, flat_size)
        columns = call(
            lambda *refs, layer=layer: map_columns(layer, rank, *refs),
            shape((locals_ * samples, fm_weight.shape[2])),
            gathered,
            fm_weight if layer else weight,
        )
        mixed = exchange(columns.reshape(locals_, samples, -1), "local", last)
        if layer + 1 < LAYERS:
            state, flat = call(
                lambda *refs, layer=layer: next_layer(layer, *refs),
                made,
                mixed,
                state,
                lin_weight,
                out_gain,
                proj,
                fm_gain,
            )
        else:
            state = call(
                lambda *refs, layer=layer: last_state(layer, *refs),
                shape((state_rows, width)),
                mixed,
                state,
                lin_weight,
                out_gain,
            )
    return state.reshape(samples, tables, width)


def solution(mesh):
    placed = (
        P(None, "local", "hst", None),
        P("hst", None, "local"),
        P(),
        P(),
        P(),
        P(),
        P(None, None, "local"),
        P(),
        P(),
        P(),
    )
    return jax.shard_map(
        shards,
        mesh=mesh,
        in_specs=placed,
        out_specs=P(("hst", "local"), None, None),
        check_vma=False,
    )
```

```python
import jax
import jax.numpy as jnp
from jax import lax
from jax.experimental import pallas as pl
from jax.experimental.pallas import tpu as pltpu
from jax.sharding import PartitionSpec as P

LAYERS = 2
PACK = 4
LOW = 256
LANES = 128
NEAR, LAST = 5, 5
SIDE = 8
FIRST, SECOND = (6, 4), (4, 4)
SMALL, MIDDLE, MORE, LARGE = 40 << 20, 49 << 20, 53 << 20, 60 << 20
F32 = jnp.float32
BF16 = jnp.bfloat16


def number(shape, axis):
    return lax.broadcasted_iota(jnp.int32, shape, axis)


def ones_where(condition):
    return jnp.where(condition, 1.0, 0.0).astype(BF16)


def matmul(a, b):
    return jnp.dot(a, b, preferred_element_type=F32)


def matmul_nt(a, b):
    return lax.dot_general(a, b, (((1,), (1,)), ((), ())), preferred_element_type=F32)


def matmul_tn(a, b):
    return lax.dot_general(a, b, (((0,), (0,)), ((), ())), preferred_element_type=F32)


def fetch(pairs, sems):
    copies = [pltpu.make_async_copy(source, target, sems.at[at]) for at, (source, target) in enumerate(pairs)]
    for copy in copies:
        copy.start()
    return copies


def local_of(rank, start):
    return (rank + start) % 8


def host_of(rank, start):
    return (rank // SIDE + start[0]) % SIDE * SIDE + (rank % SIDE + start[1]) % SIDE


def pick_rows(host_hbm, slot_hbm, stored_hbm, out_ref, host_ref, slot_ref, stored_ref, sems):
    for copy in fetch([(host_hbm, host_ref), (slot_hbm, slot_ref), (stored_hbm, stored_ref)], sems):
        copy.wait()
    tables = stored_ref.shape[0]
    holder = ones_where(host_of(number((tables, tables), 0), FIRST) == host_ref[...])
    slot = ones_where(number((tables, tables), 0) == slot_ref[...])
    chosen = matmul_nt(holder, slot).astype(BF16)
    out_ref[:, 0, :] = matmul(chosen, stored_ref[...])


def order_counts(counts_hbm, order_ref, out_ref, packed_ref, counts_ref, sems):
    copies = fetch([(counts_hbm, counts_ref)], sems)
    rows, batch = counts_ref.shape
    targets, _, length = out_ref.shape
    words = rows // PACK
    high_count = batch // LOW
    order_rows = order_ref.shape[0]
    samples = 8
    order = order_ref[...]
    parts = jnp.concatenate([order >> 8, order & (LOW - 1)], axis=0).astype(F32).astype(BF16)
    places = []
    for target in range(targets):
        m = number((1, length), 1)
        row = host_of(m // samples, SECOND) * (targets * samples)
        row = row + local_of(target, NEAR) * samples + m % samples
        found = matmul(parts, ones_where(number((LANES, length), 0) == row % LANES))
        found = jnp.where(
            number((2 * order_rows, length), 0) % order_rows == row // LANES, found, 0.0
        )
        high_part = jnp.sum(found[:order_rows], axis=0, keepdims=True).astype(jnp.int32)
        low_part = jnp.sum(found[order_rows:], axis=0, keepdims=True).astype(jnp.int32)
        places.append((high_part, low_part))
    copies[0].wait()
    word = counts_ref[0:words, :]
    for k in range(1, PACK):
        word = word + (counts_ref[k * words : (k + 1) * words, :] << (2 * k))
    word = word.astype(F32).astype(BF16)
    for high in range(high_count):
        packed_ref[high * words : (high + 1) * words, :] = word[:, high * LOW : (high + 1) * LOW]
    for target, (high_part, low_part) in enumerate(places):
        picked = matmul(packed_ref[...], ones_where(number((LOW, length), 0) == low_part))
        value = jnp.zeros((words, length), F32)
        for high in range(high_count):
            value = value + jnp.where(
                high_part == high, picked[high * words : (high + 1) * words, :], 0.0
            )
        value = value.astype(jnp.int32)
        for k in range(PACK):
            out_ref[target, k * words : (k + 1) * words, :] = (
                ((value >> (2 * k)) & 3).astype(F32).astype(BF16)
            )


def join_table(arrived_ref, ordered_ref, out_ref):
    length = ordered_ref.shape[2]
    rows = arrived_ref.shape[0]
    place = ones_where(number((rows, rows), 0) == host_of(number((rows, rows), 1), FIRST))
    table = matmul(place, arrived_ref[:, 0, :].astype(BF16)).astype(BF16)
    for target in range(out_ref.shape[0]):
        out_ref[target, :, :length] = ordered_ref[target]
        out_ref[target, :, length:] = table


def pool(both_ref, out_ref):
    length = out_ref.shape[0]
    out_ref[...] = matmul_tn(both_ref[:, :length], both_ref[:, length:]).astype(BF16)


def per_sample(matrix, samples):
    few, tables = matrix.shape
    rows, columns = few * samples, samples * tables
    tall = ones_where(number((rows, few), 0) // samples == number((rows, few), 1))
    wide = ones_where(number((1, columns), 1) % tables == number((tables, columns), 0))
    values = matmul(matmul(tall, matrix).astype(BF16), wide)
    own = number((rows, columns), 0) % samples == number((1, columns), 1) // tables
    return jnp.where(own, values, 0.0).astype(BF16)


def norm_rows(values, gain):
    mean = jnp.mean(values, axis=-1, keepdims=True)
    centered = values - mean
    spread_ = jnp.mean(centered * centered, axis=-1, keepdims=True)
    return centered * lax.rsqrt(spread_ + 1e-05) * gain


def gain_blocks(gain, rank):
    flat = gain.shape[1]
    tables = flat // rank
    own = number((1, flat), 1) % rank == number((16, flat), 0)
    row = number((flat, LANES), 0)
    least = number((1, LANES), 1) % tables * rank
    to_table = ones_where((row >= least) & (row < least + rank))
    total = jnp.zeros((16, LANES), F32)
    for _ in range(3):
        part = gain.astype(BF16).astype(F32)
        gain = gain - part
        total = total + matmul(jnp.where(own, part, 0.0).astype(BF16), to_table)
    first = number((1, LANES), 1) < tables
    return [
        jnp.where(first, total[k : k + 1], total[k + 1 : k + 2]) for k in range(0, rank, 2)
    ]


def interactions(state, proj_ref, gain_ref, layer, flat_ref):
    rows = state.shape[0]
    samples = flat_ref.shape[1]
    rank, _, tables = proj_ref.shape
    proj = jnp.concatenate(
        [proj_ref[...].astype(F32)[:, layer, :], jnp.zeros((16 - rank, tables), F32)], axis=0
    ).astype(BF16)
    proj = per_sample(proj, samples)[: rank * samples]
    gain = jnp.concatenate(gain_blocks(gain_ref[layer : layer + 1, :], rank), axis=1)
    inner = matmul(proj, state).astype(BF16)
    inter = matmul_nt(inner, state)
    own = number(inter.shape, 0) % samples == number((1, rows), 1) // tables
    inter = jnp.where(own, inter, 0.0)
    while inter.shape[1] > LANES:
        half = inter.shape[1] // 2
        inter = inter[:, :half] + inter[:, half:]
    inter = inter + pltpu.roll(inter, tables, 1)
    first = number((samples, LANES), 1) < tables
    flat = jnp.concatenate(
        [
            jnp.where(first, inter[at : at + samples], inter[at + samples : at + 2 * samples])
            for at in range(0, inter.shape[0], 2 * samples)
        ],
        axis=1,
    )
    flat = norm_rows(flat, gain).astype(BF16)
    for target in range(flat_ref.shape[0]):
        flat_ref[target] = flat


def first_layer(
    weight_hbm, moved_ref, host_ref, proj_ref, gain_ref, state_ref, flat_ref, weight_ref, sems
):
    copies = fetch([(weight_hbm.at[0], weight_ref.at[0])], sems)
    rows = state_ref.shape[0]
    tables = host_ref.shape[1]
    samples = rows // tables
    holder = ones_where(host_of(number((tables, tables), 0), SECOND) == host_ref[...])
    tall = ones_where(number((rows, tables), 0) % tables == number((rows, tables), 1))
    wide = ones_where(number((1, rows), 1) // samples == number((tables, rows), 0))
    place = matmul(matmul_nt(tall, holder).astype(BF16), wide)
    own = number((rows, rows), 0) // tables == number((1, rows), 1) % samples
    place = jnp.where(own, place, 0.0).astype(BF16)
    state = matmul(place, moved_ref[...]).astype(BF16)
    state_ref[...] = state
    interactions(state, proj_ref, gain_ref, 0, flat_ref)
    copies[0].wait()


def map_columns(layer, rank, flat_ref, weight_ref, out_ref):
    flat = flat_ref.shape[1]
    tables = flat // rank
    column = number((1, flat), 1)
    order = ones_where(
        number((flat, flat), 0) == (column % rank) * tables + column // rank
    )
    out_ref[...] = matmul(
        matmul(flat_ref[...], order).astype(BF16), weight_ref[min(layer, weight_ref.shape[0] - 1)]
    ).astype(BF16)


def next_state(layer, mixed_ref, state_ref, lin_ref, scale_ref, parts=1):
    rows, width = state_ref.shape
    sources, samples, part = mixed_ref.shape
    made = sources * part // width
    tables = rows // samples
    mixed = jnp.concatenate(
        [
            mixed_ref[(source - LAST) % sources, :, start : start + width].astype(F32)
            for source in range(sources)
            for start in range(0, part, width)
        ],
        axis=0,
    ).astype(BF16)
    column = number((1, made * samples), 1)
    turn = ones_where(
        number((made * samples, made * samples), 0)
        == (column % samples) * made + column // samples
    )
    mixed = matmul(turn, mixed)
    done = []
    share = samples // parts
    for part in range(parts):
        joined = []
        for sample in range(part * share, (part + 1) * share):
            joined.append(mixed[sample * made : (sample + 1) * made])
            joined.append(
                matmul(lin_ref[layer], state_ref[sample * tables : (sample + 1) * tables, :])
            )
        old = state_ref[part * share * tables : (part + 1) * share * tables, :]
        joined = jnp.concatenate(joined, axis=0) + old.astype(F32)
        done.append(norm_rows(joined, scale_ref[layer : layer + 1, :]).astype(BF16))
    return done


def next_layer(
    layer, mixed_ref, old_ref, lin_ref, scale_ref, proj_ref, gain_ref, state_ref, flat_ref
):
    (state,) = next_state(layer, mixed_ref, old_ref, lin_ref, scale_ref)
    state_ref[...] = state
    interactions(state, proj_ref, gain_ref, layer + 1, flat_ref)


def last_state(layer, mixed_ref, old_ref, lin_ref, scale_ref, out_hbm, part_ref, sems):
    parts, rows, _ = part_ref.shape
    copies = []
    for part, state in enumerate(
        next_state(layer, mixed_ref, old_ref, lin_ref, scale_ref, parts)
    ):
        part_ref[part] = state
        copies.append(
            pltpu.make_async_copy(
                part_ref.at[part], out_hbm.at[pl.ds(part * rows, rows)], sems.at[part]
            )
        )
        copies[-1].start()
    for copy in copies:
        copy.wait()


def call(kernel, out_shape, *args, own=(), scratch=(), flops=0, limit=SMALL, to=pltpu.VMEM):
    moved = sum(a.size * a.dtype.itemsize for a in (*own, *args))
    return pl.pallas_call(
        kernel,
        out_shape=out_shape,
        in_specs=[pl.BlockSpec(memory_space=pl.ANY)] * len(own)
        + [pl.BlockSpec(memory_space=pltpu.VMEM)] * len(args),
        out_specs=jax.tree.map(lambda _: pl.BlockSpec(memory_space=to), out_shape),
        scratch_shapes=list(scratch),
        compiler_params=pltpu.CompilerParams(vmem_limit_bytes=limit),
        cost_estimate=pl.CostEstimate(flops=flops, bytes_accessed=moved, transcendentals=0),
    )(*own, *args)


def exchange(value, axis, groups=None):
    return lax.all_to_all(value, axis, 0, 0, tiled=False, axis_index_groups=groups)


def shards(
    checkpoint,
    counts,
    table_host,
    stored_slot,
    owner_order,
    fm_proj,
    fm_weight,
    fm_gain,
    lin_weight,
    out_gain,
):
    hosts = lax.axis_size("hst")
    locals_ = lax.axis_size("local")
    width = checkpoint.shape[-1]
    tables = table_host.shape[0]
    batch = owner_order.shape[0]
    samples = batch // (hosts * locals_)
    rows = counts.shape[2]
    length = hosts * samples
    state_rows = tables * samples
    rank = fm_proj.shape[2]
    flat_size = tables * rank

    def shape(dims, dtype=BF16):
        return jax.ShapeDtypeStruct(dims, dtype)

    def fetched(*arrays):
        return [pltpu.VMEM(a.shape, a.dtype) for a in arrays]

    host = table_host.reshape(1, tables)
    picked = (host, stored_slot.reshape(1, tables), checkpoint.reshape(tables, width))
    outgoing = call(
        pick_rows,
        shape((tables, 1, width), F32),
        own=picked,
        scratch=[*fetched(*picked), pltpu.SemaphoreType.DMA((3,))],
        limit=LARGE,
    )
    arrived = exchange(outgoing, "hst", [[host_of(rank, FIRST) for rank in range(hosts)]])
    by_row = jnp.transpose(counts[0])
    ordered = call(
        order_counts,
        shape((locals_, rows, length)),
        owner_order.reshape(batch // LANES, LANES),
        own=(by_row,),
        scratch=[
            pltpu.VMEM((batch // LOW * (rows // PACK), LOW), BF16),
            *fetched(by_row),
            pltpu.SemaphoreType.DMA((1,)),
        ],
        flops=2 * batch * (LOW * LOW + 64 * LANES),
        limit=MORE,
    )
    both = exchange(
        call(join_table, shape((locals_, rows, length + width)), arrived, ordered),
        "local",
        [[local_of(rank, NEAR) for rank in range(locals_)]],
    )
    pooled = call(pool, shape((length, width)), both.reshape(locals_ * rows, length + width))
    moved = exchange(
        pooled.reshape(hosts, samples, width),
        "hst",
        [[host_of(rank, SECOND) for rank in range(hosts)]],
    )

    made = (
        shape((state_rows, width)),
        shape((locals_, samples, flat_size)),
    )
    proj = jnp.transpose(fm_proj, (2, 0, 1))
    state, flat, weight = call(
        first_layer,
        (*made, shape((1, *fm_weight.shape[1:]))),
        moved.reshape(state_rows, width),
        host,
        proj,
        fm_gain,
        own=(fm_weight,),
        scratch=[pltpu.SemaphoreType.DMA((1,))],
        limit=MIDDLE,
    )
    last = [[local_of(rank, LAST) for rank in range(locals_)]]
    for layer in range(LAYERS):
        gathered = exchange(flat, "local", last).reshape(locals_ * samples, flat_size)
        columns = call(
            lambda *refs, layer=layer: map_columns(layer, rank, *refs),
            shape((locals_ * samples, fm_weight.shape[2])),
            gathered,
            fm_weight if layer else weight,
        )
        mixed = exchange(columns.reshape(locals_, samples, -1), "local", last)
        if layer + 1 < LAYERS:
            state, flat = call(
                lambda *refs, layer=layer: next_layer(layer, *refs),
                made,
                mixed,
                state,
                lin_weight,
                out_gain,
                proj,
                fm_gain,
            )
        else:
            state = call(
                lambda *refs, layer=layer: last_state(layer, *refs),
                shape((state_rows, width)),
                mixed,
                state,
                lin_weight,
                out_gain,
                scratch=[
                    pltpu.VMEM((2, state_rows // 2, width), BF16),
                    pltpu.SemaphoreType.DMA((2,)),
                ],
                to=pl.ANY,
            )
    return state.reshape(samples, tables, width)


def solution(mesh):
    placed = (
        P(None, "local", "hst", None),
        P("hst", None, "local"),
        P(),
        P(),
        P(),
        P(),
        P(None, None, "local"),
        P(),
        P(),
        P(),
    )
    return jax.shard_map(
        shards,
        mesh=mesh,
        in_specs=placed,
        out_specs=P(("hst", "local"), None, None),
        check_vma=False,
    )
```
